32 devices in a mesh: wide: 8 (over y, x, core), narrow: 4 (over z).
Axes of the slice: x: 2, y: 2, z: 4, core: 2. Of those that a mesh axis runs over, the one named last changes fastest.
Arguments:
- gradient: float32 [2, 2048, 1024], P(None, 'wide', 'narrow'), may hold values from -6 to 6
- probe_modes: bfloat16 [4, 2, 256, 256], replicated, may hold values from -5 to 5
- mode_weights: bfloat16 [8, 4, 3, 4, 2, 256, 256], P('wide', 'narrow'), may hold values from -4 to 4
- offsets: int32 [8, 4, 3, 2], P('wide', 'narrow'), may hold values from -64 to 64, as said below
- counts: int32 [8, 4], P('wide', 'narrow'), may hold values from 1 to 3, as said below
Outputs:
- solution: float32 [2, 2048, 1024], P(None, 'wide', 'narrow')
- residual: float32 [2, 2048, 1024], P(None, 'wide', 'narrow')
The draws below stay inside these ranges and needn't reach their ends.
Inputs may be any that keep to these rules, and one draw needn't show every extreme that they name: `offsets`: each offset lies between -64 and 64; both ends are taken by some slot in every draw. `counts`: slots from a tile's count on are empty; some tile has all 3 slots live in every draw.
All inputs are finite; a program needn't handle non-finite values.
Results may differ from the reference program's by a relative error of at most 0.012.
Values sent between devices are 32-bit elements; how exact they have to be, the bound alone decides.
No kernel may reach another device: no remote copies, remote signals or barrier semaphores. Data moves between devices by JAX's collectives and lax.ppermute only.
A program may use at most 128 MiB of HBM per device.

```python
import math
import jax
import jax.numpy as jnp
from jax import lax

W = 256
MODES = 4
FCAP = 3
STEPS = 2
HALO = 64
NX = 2048
NY = 1024
N_WIDE = 8
N_NARROW = 4


def draw_offsets(key, part):
    drawn = jax.random.randint(key, (N_WIDE, N_NARROW, FCAP, 2), -HALO, HALO + 1, dtype=jnp.int32)
    chosen = jax.random.randint(jax.random.fold_in(key, 7), (), 0, N_WIDE * N_NARROW, dtype=jnp.int32)
    tile_ids = jnp.arange(N_WIDE * N_NARROW, dtype=jnp.int32).reshape(N_WIDE, N_NARROW)[:, :, None, None]
    slot_ids = jnp.arange(FCAP, dtype=jnp.int32)[None, None, :, None]
    part_ids = jnp.arange(2, dtype=jnp.int32)[None, None, None, :]
    target = (tile_ids == chosen) & (slot_ids == 0)
    drawn = jnp.where(target & (part_ids == 0), HALO, drawn)
    drawn = jnp.where(target & (part_ids == 1), -HALO, drawn)
    return drawn


def draw_counts(key, part):
    drawn = jax.random.randint(key, (N_WIDE, N_NARROW), 1, FCAP + 1, dtype=jnp.int32)
    chosen = jax.random.randint(jax.random.fold_in(key, 11), (), 0, N_WIDE * N_NARROW, dtype=jnp.int32)
    tile_ids = jnp.arange(N_WIDE * N_NARROW, dtype=jnp.int32).reshape(N_WIDE, N_NARROW)
    return jnp.where(tile_ids == chosen, FCAP, drawn)


def block_scale(stream_key, extent, cuts, smallest, largest):
    level, own = 1.0, jax.random.fold_in(stream_key, 6)
    for axis_at, shards_of in cuts:
        steps = jnp.exp(jax.random.uniform(jax.random.fold_in(own, axis_at), (shards_of,), jnp.float32, smallest / len(cuts), largest / len(cuts)))
        level = level * jnp.repeat(steps, extent[axis_at] // shards_of).reshape([-1 if axis == axis_at else 1 for axis in range(len(extent))])
    return level


def noise(own_key, dims, spread, most, shards=(), kind=jnp.bfloat16):
    values = spread * jax.random.normal(own_key, dims, jnp.float32)
    if shards:
        values = values * block_scale(own_key, dims, shards, -0.22, 0.18)
    return jnp.clip(values, -most, most).astype(kind)


def setup_inputs(seed: int = 0) -> dict:
    splits = jax.random.split(jax.random.key(seed), 6)
    return {
        "gradient": noise(splits[0], (2, NX, NY), 1.0, 6.0, ((1, 8), (2, 4)), jnp.float32),
        "probe_modes": noise(splits[1], (MODES, 2, W, W), 0.7, 5.0),
        "mode_weights": noise(splits[2], (N_WIDE, N_NARROW, FCAP, MODES, 2, W, W), 0.5, 4.0, ((0, 8), (1, 4))),
        "offsets": draw_offsets(jax.random.fold_in(splits[5], 71), 0),
        "counts": draw_counts(jax.random.fold_in(splits[5], 71), 0),
    }


damping = 0.5

def dft_tables(length, sign):
    counter = jnp.arange(length, dtype=jnp.int32)
    phases = counter[:, None] * counter[None, :] % length
    angles = phases.astype(jnp.float32) * (2.0 * math.pi / length)
    factor = 1.0 / math.sqrt(length)
    real_part = jnp.cos(angles) * factor
    imag_part = -sign * jnp.sin(angles) * factor
    left_table = jnp.stack([jnp.stack([real_part, -imag_part]), jnp.stack([imag_part, real_part])]).astype(jnp.bfloat16)
    right_table = jnp.stack([jnp.stack([real_part, imag_part]), jnp.stack([-imag_part, real_part])]).astype(jnp.bfloat16)
    return (left_table, right_table)

def left_apply(table, values):
    return jnp.einsum('pqab,nqbc->npac', table.astype(jnp.float32), values.astype(jnp.float32), precision=lax.Precision.HIGHEST)

def right_apply(table, values):
    return jnp.einsum('nqac,qpcd->npad', values.astype(jnp.float32), table.astype(jnp.float32), precision=lax.Precision.HIGHEST)

def wave_pass(patches, probe_modes, weights, live_mask, forward_tables, inverse_tables):
    frames = patches.shape[0]
    modes = probe_modes.shape[0]
    length = probe_modes.shape[-1]
    probe_re = probe_modes[None, :, 0].astype(jnp.float32)
    probe_im = probe_modes[None, :, 1].astype(jnp.float32)
    patch_re = patches[:, None, 0]
    patch_im = patches[:, None, 1]
    exit_wave = jnp.stack([probe_re * patch_re - probe_im * patch_im, probe_re * patch_im + probe_im * patch_re], axis=2).astype(jnp.bfloat16)
    stacked = exit_wave.reshape(frames * modes, 2, length, length)
    partial_value = left_apply(forward_tables[0], stacked).astype(jnp.bfloat16)
    far_field = right_apply(forward_tables[1], partial_value).reshape(frames, modes, 2, length, length)
    weight_re = weights[:, :, 0].astype(jnp.float32)
    weight_im = weights[:, :, 1].astype(jnp.float32)
    projected = lax.optimization_barrier(jnp.sum(weight_re * far_field[:, :, 0] + weight_im * far_field[:, :, 1], axis=1)) * live_mask[:, None, None]
    weighted = jnp.stack([weight_re * projected[:, None], weight_im * projected[:, None]], axis=2).astype(jnp.bfloat16)
    partial_back = left_apply(inverse_tables[0], weighted.reshape(frames * modes, 2, length, length)).astype(jnp.bfloat16)
    near_field = right_apply(inverse_tables[1], partial_back).reshape(frames, modes, 2, length, length)
    near_re = near_field[:, :, 0]
    near_im = near_field[:, :, 1]
    contribution = jnp.stack([lax.optimization_barrier(jnp.sum(probe_re * near_re + probe_im * near_im, axis=1)), lax.optimization_barrier(jnp.sum(probe_re * near_im - probe_im * near_re, axis=1))], axis=1)
    return (contribution, projected)

def apply_operator(direction, probe_modes, mode_weights, offsets, counts, forward_tables, inverse_tables):
    padded = jnp.pad(direction, ((0, 0), (HALO, HALO), (HALO, HALO)))
    tile_total = N_WIDE * N_NARROW
    weights_flat = mode_weights.reshape(tile_total, FCAP, MODES, 2, W, W)
    offsets_flat = offsets.reshape(tile_total, FCAP, 2)
    counts_flat = counts.reshape(tile_total)
    slot_ids = jnp.arange(FCAP, dtype=jnp.int32)

    def visit(total, element):
        tile_number, tile_weights, tile_offsets, tile_count = element
        row_base = tile_number // N_NARROW * W + HALO
        col_base = tile_number % N_NARROW * W + HALO
        starts = []
        pieces = []
        for slot_index in range(FCAP):
            row_start = (row_base + tile_offsets[slot_index, 0]).astype(jnp.int32)
            col_start = (col_base + tile_offsets[slot_index, 1]).astype(jnp.int32)
            starts.append((row_start, col_start))
            pieces.append(lax.dynamic_slice(padded, (jnp.int32(0), row_start, col_start), (2, W, W)))
        live_mask = (slot_ids < tile_count).astype(jnp.float32)
        contribution, projected = wave_pass(jnp.stack(pieces), probe_modes, tile_weights, live_mask, forward_tables, inverse_tables)
        for slot_index in range(FCAP):
            row_start, col_start = starts[slot_index]
            region = lax.dynamic_slice(total, (jnp.int32(0), row_start, col_start), (2, W, W))
            total = lax.dynamic_update_slice(total, region + contribution[slot_index], (jnp.int32(0), row_start, col_start))
        return (total, None)
    total, unused = lax.scan(visit, jnp.zeros_like(padded), (jnp.arange(tile_total, dtype=jnp.int32), weights_flat, offsets_flat, counts_flat))
    return total[:, HALO:HALO + NX, HALO:HALO + NY] + damping * direction

def reference(gradient, probe_modes, mode_weights, offsets, counts):
    forward_tables = dft_tables(W, 1.0)
    inverse_tables = dft_tables(W, -1.0)
    solution = jnp.zeros_like(gradient)
    residual = gradient
    direction = gradient
    norm_now = jnp.sum(residual * residual)
    for iteration in range(STEPS):
        image = apply_operator(direction, probe_modes, mode_weights, offsets, counts, forward_tables, inverse_tables)
        alpha = norm_now / jnp.sum(direction * image)
        solution = solution + alpha * direction
        residual = residual - alpha * image
        if iteration + 1 < STEPS:
            norm_next = jnp.sum(residual * residual)
            direction = residual + norm_next / norm_now * direction
            norm_now = norm_next
    return (solution, residual)
```

```python
import functools
import math

import jax
import jax.numpy as jnp
import numpy as np
from jax import lax
from jax.experimental import pallas as pl
from jax.experimental.pallas import tpu as pltpu
from jax.sharding import PartitionSpec as P

HALO = 64
SPARE = 8
damping = 0.5
F32 = jnp.float32
BF16 = jnp.bfloat16
VMEM_LIMIT = 48 * 1024 * 1024


def pairs(size, odd):
    found = []
    for i in range(odd, size - 1, 2):
        found += [(i, i + 1), (i + 1, i)]
    return found


def swap(x, axis, odd):
    wanted = pairs(lax.axis_size(axis), odd)
    if not wanted:
        return jnp.zeros_like(x)
    return lax.ppermute(x, axis, wanted)


def half_tables(length):
    counter = np.arange(length)
    angles = ((counter[:, None] * counter[None, :]) % length).astype(np.float32)
    angles = angles * np.float32(2.0 * math.pi / length)
    factor = np.float32(1.0 / math.sqrt(length))
    cos, sin = (np.cos(angles) * factor, np.sin(angles) * factor)
    half = length // 2
    tables = []
    for parity in (0, 1):
        c, s = (cos[parity::2, :half], sin[parity::2, :half])
        left = np.concatenate([np.concatenate([c, s], 1), np.concatenate([-s, c], 1)], 0)
        tables += [left, left.T]
    return jnp.asarray(np.stack(tables), BF16)


def sorting_tables(length):
    order = np.concatenate([np.arange(0, length, 2), np.arange(1, length, 2)])
    left = np.zeros((length, length), np.float32)
    left[np.arange(length), order] = 1.0
    return jnp.asarray(np.stack([left, left.T]), BF16)


def dot(a, b):
    return jnp.dot(a, b, preferred_element_type=F32)


def cat(parts, axis):
    return jnp.concatenate(parts, axis=axis)


def lanes_low(shape):
    return lax.broadcasted_iota(jnp.int32, shape, len(shape) - 1) < shape[-1] // 2


def forward(xr, xi, te, te_t, to, to_t):
    h = xr.shape[0] // 2
    even = cat([xr[:h] + xr[h:], xi[:h] + xi[h:]], 0).astype(BF16)
    odd = cat([xr[:h] - xr[h:], xi[:h] - xi[h:]], 0).astype(BF16)
    ye, yo = (dot(te, even), dot(to, odd))
    plus, minus = ([], [])
    for y in (ye, yo):
        yr, yi = (y[:h], y[h:])
        plus.append(cat([yr[:, :h] + yr[:, h:], yi[:, :h] + yi[:, h:]], 1))
        minus.append(cat([yr[:, :h] - yr[:, h:], yi[:, :h] - yi[:, h:]], 1))
    ze = dot(cat(plus, 0).astype(BF16), te_t)
    zo = dot(cat(minus, 0).astype(BF16), to_t)
    return (ze, zo)


def inverse(ve, vo, te, te_t, to, to_t):
    h = ve.shape[0] // 2
    top = cat([cat([ve[:h, :h], vo[:h, :h]], 1), cat([ve[:h, h:], vo[:h, h:]], 1)], 0)
    low = cat([cat([ve[h:, :h], vo[h:, :h]], 1), cat([ve[h:, h:], vo[h:, h:]], 1)], 0)
    a, b = (dot(te_t, top), dot(to_t, low))
    s, d = (a + b, a - b)
    le = cat([cat([s[:h, :h], s[h:, :h]], 1), cat([d[:h, :h], d[h:, :h]], 1)], 0).astype(BF16)
    lo = cat([cat([s[:h, h:], s[h:, h:]], 1), cat([d[:h, h:], d[h:, h:]], 1)], 0).astype(BF16)
    p, q = (dot(le, te), dot(lo, to))
    s, d = (p + q, p - q)
    return (cat([s[:, :h], d[:, :h]], 1), cat([s[:, h:], d[:, h:]], 1))


def shifted_place(offsets, k, span):
    row = HALO + offsets[2 * k]
    col = offsets[2 * k + 1]
    group = pl.multiple_of(row // 8 * 8, 8)
    blocks = span // 128
    first = jnp.where(col < 0, blocks - 1, 0)
    places = [
        pl.multiple_of(lax.rem(first + i, blocks) * 128, 128) for i in range(blocks)
    ]
    return (group, row - group, places, jnp.where(col < 0, col + 128, col))


def take_patch(ext, offsets, k, width, patch):
    group, down, places, across = shifted_place(offsets, k, ext.shape[2])
    groups = width // 8
    sub = lax.broadcasted_iota(jnp.int32, (groups, 8, 128), 1)
    lane = lax.broadcasted_iota(jnp.int32, (width, 128), 1)
    for q in range(2):
        turned = []
        for place in places:
            x = ext[q, pl.ds(group, width + 8), pl.ds(place, 128)].reshape(groups + 1, 8, 128)
            x = pltpu.roll(x, lax.rem(8 - down, 8), 1)
            x = jnp.where(sub < 8 - down, x[:-1], x[1:]).reshape(width, 128)
            turned.append(pltpu.roll(x, lax.rem(128 - across, 128), 1))
        for i in range(width // 128):
            patch[q, :, 128 * i : 128 * (i + 1)] = jnp.where(
                lane < 128 - across, turned[i], turned[i + 1]
            )


def project(patch, probe, weights, k, tables):
    te, te_t, to, to_t = (tables[i] for i in range(4))
    xr, xi = (patch[0], patch[1])
    width = xr.shape[0]
    h = width // 2
    total_e = total_o = None
    for m in range(probe.shape[0]):
        pr, pi = (probe[m, 0].astype(F32), probe[m, 1].astype(F32))
        ze, zo = forward(pr * xr - pi * xi, pr * xi + pi * xr, te, te_t, to, to_t)
        ze = ze * weights[k, m, :, :width].astype(F32)
        zo = zo * weights[k, m, :, width:].astype(F32)
        total_e = ze if m == 0 else total_e + ze
        total_o = zo if m == 0 else total_o + zo
    return (total_e[:, :h] + total_e[:, h:], total_o[:, :h] + total_o[:, h:])


def back_project(pe, po, probe, weights, k, tables):
    te, te_t, to, to_t = (tables[i] for i in range(4))
    width = pe.shape[0]
    pe2, po2 = (cat([pe, pe], 1), cat([po, po], 1))
    cr = ci = None
    for m in range(probe.shape[0]):
        ve = (weights[k, m, :, :width].astype(F32) * pe2).astype(BF16)
        vo = (weights[k, m, :, width:].astype(F32) * po2).astype(BF16)
        nr, ni = inverse(ve, vo, te, te_t, to, to_t)
        pr, pi = (probe[m, 0].astype(F32), probe[m, 1].astype(F32))
        r = pr * nr + pi * ni
        i = pr * ni - pi * nr
        cr = r if m == 0 else cr + r
        ci = i if m == 0 else ci + i
    return (cr, ci)


def put_patch(total, offsets, k, parts):
    width = parts[0].shape[0]
    group, down, places, across = shifted_place(offsets, k, total.shape[2])
    groups = width // 8
    sub = lax.broadcasted_iota(jnp.int32, (groups + 1, 8, 128), 1)
    lane = lax.broadcasted_iota(jnp.int32, (width + 8, 128), 1)
    none = jnp.zeros((1, 8, 128), F32)
    for q in range(2):
        turned = [jnp.zeros((width + 8, 128), F32)]
        for i in range(width // 128):
            x = parts[q][:, 128 * i : 128 * (i + 1)].reshape(groups, 8, 128)
            x = pltpu.roll(x, down, 1)
            x = jnp.where(sub < down, cat([none, x], 0), cat([x, none], 0))
            turned.append(pltpu.roll(x.reshape(width + 8, 128), across, 1))
        turned.append(turned[0])
        for i, place in enumerate(places):
            total[q, pl.ds(group, width + 8), pl.ds(place, 128)] += jnp.where(
                lane < across, turned[i], turned[i + 1]
            )


def square_sum(x):
    return jnp.sum(x * x)


def scalar_tile(values):
    rows = lax.broadcasted_iota(jnp.int32, (8, 128), 0)
    tile = jnp.zeros((8, 128), F32)
    for i, value in enumerate(values):
        tile = jnp.where(rows == i, value, tile)
    return tile


def parity_of(axis):
    return lax.rem(lax.axis_index(axis), 2)


def by_parity(axis, low, high, first, second):
    even = parity_of(axis) == 0

    @pl.when(even)
    def _():
        first(high())
        second(low())

    @pl.when(jnp.logical_not(even))
    def _():
        first(low())
        second(high())


def store(ref):
    def put(value):
        ref[...] = value

    return put


def halo_rows_kernel(g, first, second):
    n = g.shape[1]
    by_parity(
        "wide", lambda: g[:, :HALO], lambda: g[:, n - HALO :], store(first), store(second)
    )


def strip_low(x, width):
    low = lanes_low((x.shape[1], 2 * HALO))
    re, im = (x[0, :, : 2 * HALO], x[1, :, : 2 * HALO])
    return jnp.where(low, re, pltpu.roll(im, HALO, 1))


def strip_high(x, width):
    low = lanes_low((x.shape[1], 2 * HALO))
    re, im = (x[0, :, width - 2 * HALO : width], x[1, :, width - 2 * HALO : width])
    return jnp.where(low, pltpu.roll(im, HALO, 1), re)


def fill_rows(ext, g, first, second):
    n, width = (g.shape[1], g.shape[2])
    even = parity_of("wide") == 0
    above = jnp.where(even, second[...], first[...])
    below = jnp.where(even, first[...], second[...])
    ext[:, :HALO, :width] = above
    ext[:, HALO : HALO + n, :width] = g[...]
    ext[:, HALO + n : 2 * HALO + n, :width] = below


def halo_cols_kernel(g, first, second, out_first, out_second, ext):
    width = g.shape[2]
    fill_rows(ext, g, first, second)
    by_parity(
        "narrow",
        lambda: strip_low(ext, width),
        lambda: strip_high(ext, width),
        store(out_first),
        store(out_second),
    )


def fill_cols(ext, width, first, second):
    even = parity_of("narrow") == 0
    right = jnp.where(even, first[...], second[...])
    left = jnp.where(even, second[...], first[...])
    low = lanes_low(right.shape)
    tall = right.shape[0]
    ext[0, :tall, width:] = jnp.where(low, right, left)
    ext[1, :tall, width:] = pltpu.roll(jnp.where(low, left, right), HALO, 1)


def sort_weights_kernel(w, sorter, out):
    width = w.shape[-1]
    h = width // 2
    re = dot(dot(sorter[0], w[0, 0, 0]).astype(BF16), sorter[1])
    im = dot(dot(sorter[0], w[0, 0, 1]).astype(BF16), sorter[1])
    out[0, 0] = cat([re[:, :h], im[:, :h], re[:, h:], im[:, h:]], 1).astype(BF16)


def first_pass_kernel(
    count, offsets, g, row1, row2, col1, col2, probe, weights, tables,
    total, sums, sr1, sr2, si1, si2, ext, patch,
):
    width = g.shape[2]
    fill_rows(ext, g, row1, row2)
    fill_cols(ext, width, col1, col2)
    total[...] = jnp.zeros_like(total)

    def visit(k, energy):
        take_patch(ext, offsets, k, width, patch)
        pe, po = project(patch, probe, weights, k, tables)
        put_patch(total, offsets, k, back_project(pe, po, probe, weights, k, tables))
        return energy + square_sum(pe) + square_sum(po)

    energy = lax.fori_loop(0, count[0], visit, F32(0.0))
    sums[...] = scalar_tile([square_sum(g[...]), energy])
    send_row_bands(total, 0, sr1, sr2)
    send_col_bands(total, 1, si1, si2)


def send_row_bands(total, q, first, second):
    n = total.shape[1] - SPARE
    by_parity(
        "wide",
        lambda: total[q, : 2 * HALO],
        lambda: total[q, n - 2 * HALO : n],
        store(first),
        store(second),
    )


def send_col_bands(total, q, first, second):
    n = total.shape[1] - SPARE
    width = total.shape[2] - 2 * HALO
    low = lanes_low((n, 2 * HALO))
    by_parity(
        "narrow",
        lambda: jnp.where(low, total[q, :n, : 2 * HALO], total[q, :n, width:]),
        lambda: jnp.where(low, total[q, :n, width:], total[q, :n, width - 2 * HALO : width]),
        store(first),
        store(second),
    )


def add_row_bands(total, q, first, second):
    n = total.shape[1] - SPARE
    even = parity_of("wide") == 0
    total[q, : 2 * HALO] += jnp.where(even, second[...], first[...])
    total[q, n - 2 * HALO : n] += jnp.where(even, first[...], second[...])


def add_col_bands(total, q, first, second):
    n = total.shape[1] - SPARE
    width = total.shape[2] - 2 * HALO
    even = parity_of("narrow") == 0
    right = jnp.where(even, first[...], second[...])
    left = jnp.where(even, second[...], first[...])
    low = lanes_low(right.shape)
    total[q, :n, width:] += jnp.where(low, right, left)
    total[q, :n, : 2 * HALO] += jnp.where(low, left, 0.0)
    total[q, :n, width - 2 * HALO : width] += jnp.where(low, 0.0, right)


def bands_kernel(total, rr1, rr2, ri1, ri2, out, sr1, sr2, si1, si2):
    out[...] = total[...]
    add_row_bands(out, 0, rr1, rr2)
    add_col_bands(out, 1, ri1, ri2)
    send_col_bands(out, 0, sr1, sr2)
    send_row_bands(out, 1, si1, si2)


def second_forward_kernel(
    last_row, last_col, count, offsets, total, rr1, rr2, ri1, ri2, sums, probe, weights, tables,
    image, projected, all_sums, ext, patch,
):
    width = image.shape[2]
    n = total.shape[1] - SPARE
    ext[...] = total[...]
    add_col_bands(ext, 0, rr1, rr2)
    add_row_bands(ext, 1, ri1, ri2)

    @pl.when(lax.axis_index("wide") == 0)
    def _():
        ext[:, :HALO] = jnp.zeros((2, HALO, ext.shape[2]), F32)

    @pl.when(lax.axis_index("wide") == last_row)
    def _():
        ext[:, n - HALO : n] = jnp.zeros((2, HALO, ext.shape[2]), F32)

    low = lanes_low((2, n, 2 * HALO))
    @pl.when(lax.axis_index("narrow") == 0)
    def _():
        ext[:, :n, width:] = jnp.where(low, ext[:, :n, width:], 0.0)

    @pl.when(lax.axis_index("narrow") == last_col)
    def _():
        ext[:, :n, width:] = jnp.where(low, 0.0, ext[:, :n, width:])

    core = ext[:, HALO : n - HALO, :width]
    image[...] = core

    def visit(k, energy):
        take_patch(ext, offsets, k, width, patch)
        pe, po = project(patch, probe, weights, k, tables)
        projected[k] = cat([pe, po], 1)
        return energy + square_sum(pe) + square_sum(po)

    energy = lax.fori_loop(0, count[0], visit, F32(0.0))
    rows = lax.broadcasted_iota(jnp.int32, (8, 128), 0)
    all_sums[...] = jnp.where(
        rows == 2, square_sum(core), jnp.where(rows == 3, energy, sums[...])
    )


def second_backward_kernel(
    count, offsets, projected, probe, weights, tables, total, first, second
):
    total[...] = jnp.zeros_like(total)
    h = projected.shape[2] // 2
    n = total.shape[1] - SPARE

    def visit(k, carried):
        pe, po = (projected[k, :, :h], projected[k, :, h:])
        put_patch(total, offsets, k, back_project(pe, po, probe, weights, k, tables))
        return carried

    lax.fori_loop(0, count[0], visit, 0)
    by_parity(
        "wide",
        lambda: total[:, :HALO],
        lambda: total[:, n - HALO : n],
        store(first),
        store(second),
    )


def fold_rows_kernel(total, first, second, middle, out_first, out_second):
    n = middle.shape[1]
    width = middle.shape[2] - 2 * HALO
    even = parity_of("wide") == 0
    middle[...] = total[:, HALO : HALO + n]
    middle[:, :HALO] += jnp.where(even, second[...], first[...])
    middle[:, n - HALO :] += jnp.where(even, first[...], second[...])
    low = lanes_low((n, 2 * HALO))
    re, im = (middle[0, :, width:], middle[1, :, width:])
    im = pltpu.roll(im, HALO, 1)
    by_parity(
        "narrow",
        lambda: jnp.where(low, im, re),
        lambda: jnp.where(low, re, im),
        store(out_first),
        store(out_second),
    )


def finish_kernel(g, image, middle, first, second, sums, solved, left_over):
    width = g.shape[2]
    even = parity_of("narrow") == 0
    right = jnp.where(even, first[...], second[...])
    left = jnp.where(even, second[...], first[...])
    low = lanes_low(right.shape)
    n0, s0, uu, s1 = (sums[i : i + 1, :1] for i in range(4))
    mu = s0 / n0
    a0 = n0 / (s0 + damping * n0)
    n1 = a0 * a0 * (uu - mu * s0)
    b = n1 / n0
    c1 = a0 * mu + b
    curve = damping * (n1 + b * b * n0) + c1 * c1 * s0 - 2.0 * c1 * a0 * uu + a0 * a0 * s1
    a1 = n1 / curve
    for q in range(2):
        u = image[q]
        v = middle[q, :, :width]
        if q == 0:
            low_part, high_part = (left, right)
        else:
            low_part, high_part = (pltpu.roll(left, HALO, 1), pltpu.roll(right, HALO, 1))
        v = cat(
            [
                v[:, : 2 * HALO] + jnp.where(low, low_part, 0.0),
                v[:, 2 * HALO : width - 2 * HALO],
                v[:, width - 2 * HALO :] + jnp.where(low, 0.0, high_part),
            ],
            1,
        ) if width > 4 * HALO else cat(
            [
                v[:, : 2 * HALO] + jnp.where(low, low_part, 0.0),
                v[:, width - 2 * HALO :] + jnp.where(low, 0.0, high_part),
            ],
            1,
        )
        d1 = c1 * g[q] - a0 * u
        r1 = a0 * (mu * g[q] - u)
        solved[q] = a0 * g[q] + a1 * d1
        left_over[q] = r1 - a1 * (damping * d1 + c1 * u - a0 * v)


def reduce_all(x):
    for axis in ("wide", "narrow"):
        size = lax.axis_size(axis)
        if size & (size - 1):
            x = lax.psum(x, axis)
            continue
        step = 1
        while step < size:
            x = x + lax.ppermute(x, axis, [(i, i ^ step) for i in range(size)])
            step *= 2
    return x


def shape(*dims):
    return jax.ShapeDtypeStruct(dims, F32)


def call(kernel, outs, smem, args, scratch=(), flops=0):
    specs = [pl.BlockSpec(memory_space=pltpu.SMEM)] * smem
    specs += [pl.BlockSpec(memory_space=pltpu.VMEM)] * (len(args) - smem)
    moved = sum(a.size * a.dtype.itemsize for a in args) + sum(4 * o.size for o in outs)
    return pl.pallas_call(
        kernel,
        out_shape=outs,
        in_specs=specs,
        out_specs=[pl.BlockSpec(memory_space=pltpu.VMEM)] * len(outs),
        scratch_shapes=list(scratch),
        compiler_params=pltpu.CompilerParams(vmem_limit_bytes=VMEM_LIMIT),
        cost_estimate=pl.CostEstimate(flops=flops, bytes_accessed=moved, transcendentals=0),
    )(*args)


def sort_weights(w):
    slots, modes, parts, rows, cols = w.shape
    return pl.pallas_call(
        sort_weights_kernel,
        out_shape=jax.ShapeDtypeStruct((slots, modes, rows, parts * cols), BF16),
        grid=(slots, modes),
        in_specs=[
            pl.BlockSpec((1, 1, parts, rows, cols), lambda k, m: (k, m, 0, 0, 0)),
            pl.BlockSpec((2, rows, cols), lambda k, m: (0, 0, 0)),
        ],
        out_specs=pl.BlockSpec((1, 1, rows, parts * cols), lambda k, m: (k, m, 0, 0)),
        cost_estimate=pl.CostEstimate(
            flops=8 * slots * modes * rows * cols * rows,
            bytes_accessed=4 * w.size,
            transcendentals=0,
        ),
    )(w, sorting_tables(cols))


def local(gradient, probe_modes, mode_weights, offsets, counts):
    weights = mode_weights[0, 0]
    slots, modes = weights.shape[:2]
    rows, width = gradient.shape[1:]
    tall, broad = (rows + 2 * HALO, width + 2 * HALO)
    stored = tall + SPARE
    offsets = offsets.reshape(-1)
    counts = counts.reshape(-1)
    tables = half_tables(width)
    pass_flops = 8 * 2 * slots * modes * 2 * width * width * width
    extended = pltpu.VMEM((2, stored, broad), F32)
    patch = pltpu.VMEM((2, rows, width), F32)

    row_sends = call(halo_rows_kernel, [shape(2, HALO, width)] * 2, 0, [gradient])
    row1, row2 = (swap(x, "wide", i) for i, x in enumerate(row_sends))
    sorted_weights = sort_weights(weights)
    col_sends = call(
        halo_cols_kernel, [shape(tall, 2 * HALO)] * 2, 0, [gradient, row1, row2],
        [pltpu.VMEM((2, tall, width), F32)],
    )
    col1, col2 = (swap(x, "narrow", i) for i, x in enumerate(col_sends))

    row_band, col_band = (shape(2 * HALO, broad), shape(tall, 2 * HALO))
    total, sums, sr1, sr2, si1, si2 = call(
        first_pass_kernel,
        [shape(2, stored, broad), shape(8, 128), row_band, row_band, col_band, col_band],
        2,
        [counts, offsets, gradient, row1, row2, col1, col2, probe_modes, sorted_weights, tables],
        [extended, patch],
        pass_flops,
    )
    total, sr1, sr2, si1, si2 = call(
        bands_kernel,
        [shape(2, stored, broad), col_band, col_band, row_band, row_band],
        0,
        [total, swap(sr1, "wide", 0), swap(sr2, "wide", 1), swap(si1, "narrow", 0), swap(si2, "narrow", 1)],
    )
    image, projected, sums = call(
        functools.partial(
            second_forward_kernel, lax.axis_size("wide") - 1, lax.axis_size("narrow") - 1
        ),
        [shape(2, rows, width), shape(slots, rows, width), shape(8, 128)],
        2,
        [
            counts, offsets, total,
            swap(sr1, "narrow", 0), swap(sr2, "narrow", 1), swap(si1, "wide", 0), swap(si2, "wide", 1),
            sums, probe_modes, sorted_weights, tables,
        ],
        [extended, patch],
        pass_flops // 2,
    )
    sums = reduce_all(sums)
    total, f1, f2 = call(
        second_backward_kernel,
        [shape(2, stored, broad), shape(2, HALO, broad), shape(2, HALO, broad)],
        2,
        [counts, offsets, projected, probe_modes, sorted_weights, tables],
        [],
        pass_flops // 2,
    )
    middle, f1, f2 = call(
        fold_rows_kernel,
        [shape(2, rows, broad), shape(rows, 2 * HALO), shape(rows, 2 * HALO)],
        0,
        [total, swap(f1, "wide", 0), swap(f2, "wide", 1)],
    )
    solved, left_over = call(
        finish_kernel,
        [shape(2, rows, width)] * 2,
        0,
        [gradient, image, middle, swap(f1, "narrow", 0), swap(f2, "narrow", 1), sums],
    )
    return (solved, left_over)


def solution(mesh):
    placed = (
        P(None, "wide", "narrow"),
        P(),
        P("wide", "narrow", None, None, None, None, None),
        P("wide", "narrow", None, None),
        P("wide", "narrow"),
    )
    return jax.shard_map(
        local,
        mesh=mesh,
        in_specs=placed,
        out_specs=(P(None, "wide", "narrow"), P(None, "wide", "narrow")),
        check_vma=False,
    )
```

```python
import functools
import math

import jax
import jax.numpy as jnp
import numpy as np
from jax import lax
from jax.experimental import pallas as pl
from jax.experimental.pallas import tpu as pltpu
from jax.sharding import PartitionSpec as P

HALO = 64
damping = 0.5
F32 = jnp.float32
BF16 = jnp.bfloat16
MIB = 1024 * 1024


def pairs(size, odd):
    found = []
    for i in range(odd, size - 1, 2):
        found += [(i, i + 1), (i + 1, i)]
    return found


def swap(x, axis, odd):
    wanted = pairs(lax.axis_size(axis), odd)
    if not wanted:
        return jnp.zeros_like(x)
    return lax.ppermute(x, axis, wanted)


def half_tables(length):
    counter = np.arange(length)
    angles = ((counter[:, None] * counter[None, :]) % length).astype(np.float32)
    angles = angles * np.float32(2.0 * math.pi / length)
    factor = np.float32(1.0 / math.sqrt(length))
    cos, sin = (np.cos(angles) * factor, np.sin(angles) * factor)
    half = length // 2
    tables = []
    for parity in (0, 1):
        c, s = (cos[parity::2, :half], sin[parity::2, :half])
        left = np.concatenate([np.concatenate([c, s], 1), np.concatenate([-s, c], 1)], 0)
        tables += [left, left.T]
    return jnp.asarray(np.stack(tables), BF16)


def sorting_tables(length):
    order = np.concatenate([np.arange(0, length, 2), np.arange(1, length, 2)])
    left = np.zeros((length, length), np.float32)
    left[np.arange(length), order] = 1.0
    return jnp.asarray(np.stack([left, left.T]), BF16)


def dot(a, b):
    return jnp.dot(a, b, preferred_element_type=F32)


def cat(parts, axis):
    return jnp.concatenate(parts, axis=axis)


def lanes_low(shape):
    return lax.broadcasted_iota(jnp.int32, shape, len(shape) - 1) < shape[-1] // 2


def shifted_place(frames, k, blocks):
    row = HALO + frames[1 + k]
    col = frames[1 + frames.shape[0] // 2 + k]
    first = jnp.where(col < 0, blocks - 1, 0)
    places = [lax.rem(first + i, blocks) for i in range(blocks)]
    return (row, places, jnp.where(col < 0, col + 128, col))


def take_patch(ext, frames, k, patch):
    width = patch.shape[1]
    row, places, across = shifted_place(frames, k, ext.shape[1])
    lane = lax.broadcasted_iota(jnp.int32, (width, 128), 1)
    back = lax.rem(128 - across, 128)
    for q in range(2):
        found = [ext[q, place, pl.ds(row, width), :] for place in places]
        for i in range(width // 128):
            both = jnp.where(lane >= across, found[i], found[i + 1])
            patch[q, :, 128 * i : 128 * (i + 1)] = pltpu.roll(both, back, 1)


def put_patch(total, frames, k, parts):
    width = parts[0].shape[0]
    row, places, across = shifted_place(frames, k, total.shape[1])
    lane = lax.broadcasted_iota(jnp.int32, (width, 128), 1)
    none = jnp.zeros((width, 128), F32)
    for q in range(2):
        turned = [none]
        for i in range(width // 128):
            turned.append(pltpu.roll(parts[q][:, 128 * i : 128 * (i + 1)], across, 1))
        turned.append(none)
        for i, place in enumerate(places):
            total[q, place, pl.ds(row, width), :] += jnp.where(
                lane < across, turned[i], turned[i + 1]
            )


def project(patch, probe, weights, k, tables, stage):
    te, te_t, to, to_t = (tables[i] for i in range(4))
    xr, xi = (patch[0], patch[1])
    width = xr.shape[0]
    h = width // 2
    modes = probe.shape[0]
    for m in range(modes):
        pr, pi = (probe[m, 0].astype(F32), probe[m, 1].astype(F32))
        er, ei = (pr * xr - pi * xi, pr * xi + pi * xr)
        even = cat([er[:h] + er[h:], ei[:h] + ei[h:]], 0).astype(BF16)
        odd = cat([er[:h] - er[h:], ei[:h] - ei[h:]], 0).astype(BF16)
        for e, y in enumerate((dot(te, even), dot(to, odd))):
            yr, yi = (y[:h], y[h:])
            plus = cat([yr[:, :h] + yr[:, h:], yi[:, :h] + yi[:, h:]], 1)
            minus = cat([yr[:, :h] - yr[:, h:], yi[:, :h] - yi[:, h:]], 1)
            stage[0, m, e * h : (e + 1) * h] = plus.astype(BF16)
            stage[1, m, e * h : (e + 1) * h] = minus.astype(BF16)
    found = []
    for e, table in enumerate((te_t, to_t)):
        acc = None
        for m in range(modes):
            z = dot(stage[e, m], table)
            z = z * weights[k, m, :, e * width : (e + 1) * width].astype(F32)
            acc = z if m == 0 else acc + z
        found.append(acc[:, :h] + acc[:, h:])
    return tuple(found)


def back_project(pe, po, probe, weights, k, tables, stage):
    te, te_t, to, to_t = (tables[i] for i in range(4))
    width = pe.shape[0]
    h = width // 2
    modes = probe.shape[0]
    pe2, po2 = (cat([pe, pe], 1), cat([po, po], 1))
    for m in range(modes):
        ve = (weights[k, m, :, :width].astype(F32) * pe2).astype(BF16)
        vo = (weights[k, m, :, width:].astype(F32) * po2).astype(BF16)
        top = cat([cat([ve[:h, :h], vo[:h, :h]], 1), cat([ve[:h, h:], vo[:h, h:]], 1)], 0)
        low = cat([cat([ve[h:, :h], vo[h:, :h]], 1), cat([ve[h:, h:], vo[h:, h:]], 1)], 0)
        a, b = (dot(te_t, top), dot(to_t, low))
        s, d = (a + b, a - b)
        for e, c in enumerate((slice(0, h), slice(h, width))):
            stage[e, m, :h] = cat([s[:h, c], s[h:, c]], 1).astype(BF16)
            stage[e, m, h:] = cat([d[:h, c], d[h:, c]], 1).astype(BF16)
    cr = ci = None
    for m in range(modes):
        a, b = (dot(stage[0, m], te), dot(stage[1, m], to))
        s, d = (a + b, a - b)
        nr, ni = (cat([s[:, :h], d[:, :h]], 1), cat([s[:, h:], d[:, h:]], 1))
        pr, pi = (probe[m, 0].astype(F32), probe[m, 1].astype(F32))
        r = pr * nr + pi * ni
        i = pr * ni - pi * nr
        cr = r if m == 0 else cr + r
        ci = i if m == 0 else ci + i
    return (cr, ci)


def square_sum(x):
    return jnp.sum(x * x)


def scalar_tile(values):
    rows = lax.broadcasted_iota(jnp.int32, (8, 128), 0)
    tile = jnp.zeros((8, 128), F32)
    for i, value in enumerate(values):
        tile = jnp.where(rows == i, value, tile)
    return tile


def parity_of(axis):
    return lax.rem(lax.axis_index(axis), 2)


def by_parity(axis, low, high, first, second):
    even = parity_of(axis) == 0

    @pl.when(even)
    def _():
        first(high())
        second(low())

    @pl.when(jnp.logical_not(even))
    def _():
        first(low())
        second(high())


def lower_upper(axis, first, second):
    even = parity_of(axis) == 0
    return (jnp.where(even, second, first), jnp.where(even, first, second))


def store(ref):
    def put(value):
        ref[...] = value

    return put


def halo_rows_kernel(g, first, second, arrived):
    n = g.shape[1]

    low, high = (g.at[:, :HALO], g.at[:, n - HALO :])
    by_parity(
        "wide",
        lambda: low,
        lambda: high,
        lambda source: pltpu.make_async_copy(source, first, arrived.at[0]).start(),
        lambda source: pltpu.make_async_copy(source, second, arrived.at[1]).start(),
    )
    pltpu.make_async_copy(low, first, arrived.at[0]).wait()
    pltpu.make_async_copy(low, second, arrived.at[1]).wait()


def fill_rows(ext, g, first, second):
    n, width = (g.shape[1], g.shape[2])
    above, below = lower_upper("wide", first[...], second[...])
    for b in range(width // 128):
        cols = slice(128 * b, 128 * (b + 1))
        ext[:, b, :HALO] = above[:, :, cols]
        ext[:, b, HALO : HALO + n] = g[:, :, cols]
        ext[:, b, HALO + n :] = below[:, :, cols]


def halo_cols_kernel(second, first, g, out_first, out_second, ext):
    last = g.shape[2] // 128 - 1
    fill_rows(ext, g, first, second)
    low = lanes_low(out_first.shape)
    by_parity(
        "narrow",
        lambda: jnp.where(low, ext[0, 0], pltpu.roll(ext[1, 0], HALO, 1)),
        lambda: jnp.where(low, pltpu.roll(ext[1, last], HALO, 1), ext[0, last]),
        store(out_first),
        store(out_second),
    )


def fill_cols(ext, first, second):
    left, right = lower_upper("narrow", first[...], second[...])
    last = ext.shape[1] - 1
    low = lanes_low(right.shape)
    ext[0, last] = jnp.where(low, right, left)
    ext[1, last] = pltpu.roll(jnp.where(low, left, right), HALO, 1)


def sort_weights(frames, w, sorter, out, held, arrived, begin, end, meanwhile):
    width = w.shape[-1]
    h = width // 2
    modes = w.shape[1]

    def fetch(k):
        return pltpu.make_async_copy(w.at[k], held.at[k], arrived.at[k])

    for k in range(begin, end):

        @pl.when(k < frames[0])
        def _():
            fetch(k).start()

    meanwhile()

    def visit(k, carried):
        fetch(k).wait()
        for m in range(modes):
            re = dot(dot(sorter[0], held[k, m, 0]).astype(BF16), sorter[1])
            im = dot(dot(sorter[0], held[k, m, 1]).astype(BF16), sorter[1])
            out[k, m] = cat([re[:, :h], im[:, :h], re[:, h:], im[:, h:]], 1).astype(BF16)
        return carried

    lax.fori_loop(begin, jnp.minimum(end, frames[0]), visit, 0)


def prepare_kernel(
    frames, w, sorter_far, probe_far, tables_far, g_far,
    out, sorter, probe, tables, g, held, arrived, loaded,
):
    moves = ((sorter_far, sorter), (g_far, g), (probe_far, probe), (tables_far, tables))
    moves = [pltpu.make_async_copy(a, b, loaded.at[i]) for i, (a, b) in enumerate(moves)]
    moves[0].start()

    def meanwhile():
        for move in moves[1:]:
            move.start()
        moves[0].wait()

    sort_weights(frames, w, sorter, out, held, arrived, 0, 1, meanwhile)
    for move in moves[1:]:
        move.wait()


def prepare_rest_kernel(frames, w, sorter, first, out, held, arrived):
    sort_weights(frames, w, sorter, out, held, arrived, 1, w.shape[0], lambda: None)


def first_pass_kernel(
    frames, g, row1, row2, col1, col2, probe, weights, tables,
    total, sums, sr1, sr2, si1, si2, ext, patch, stage,
):
    fill_rows(ext, g, row1, row2)
    fill_cols(ext, col1, col2)
    total[...] = jnp.zeros_like(total)

    def visit(k, energy):
        take_patch(ext, frames, k, patch)
        pe, po = project(patch, probe, weights, k, tables, stage)
        put_patch(total, frames, k, back_project(pe, po, probe, weights, k, tables, stage))
        return energy + square_sum(pe) + square_sum(po)

    energy = lax.fori_loop(0, frames[0], visit, F32(0.0))
    sums[...] = scalar_tile([square_sum(g[...]), energy])
    send_row_bands(total, 0, sr1, sr2)
    send_col_bands(total, 1, si1, si2)


def send_row_bands(total, q, first, second):
    n = total.shape[2]
    by_parity(
        "wide",
        lambda: total[q, :, : 2 * HALO].reshape(first.shape),
        lambda: total[q, :, n - 2 * HALO :].reshape(first.shape),
        store(first),
        store(second),
    )


def send_col_bands(total, q, first, second):
    last = total.shape[1] - 1
    low = lanes_low(first.shape)
    by_parity(
        "narrow",
        lambda: jnp.where(low, total[q, 0], total[q, last]),
        lambda: jnp.where(low, total[q, last], total[q, last - 1]),
        store(first),
        store(second),
    )


def add_row_bands(total, q, first, second):
    blocks, n = total.shape[1:3]
    above, below = lower_upper("wide", first[...], second[...])
    total[q, :, : 2 * HALO] += above.reshape(blocks, 2 * HALO, 128)
    total[q, :, n - 2 * HALO :] += below.reshape(blocks, 2 * HALO, 128)


def add_col_bands(total, q, first, second):
    last = total.shape[1] - 1
    left, right = lower_upper("narrow", first[...], second[...])
    low = lanes_low(right.shape)
    total[q, last] += jnp.where(low, right, left)
    total[q, 0] += jnp.where(low, left, 0.0)
    total[q, last - 1] += jnp.where(low, 0.0, right)


def bands_kernel(rr2, ri1, ri2, rr1, total, out, sr1, sr2, si1, si2):
    add_row_bands(out, 0, rr1, rr2)
    add_col_bands(out, 1, ri1, ri2)
    send_col_bands(out, 0, sr1, sr2)
    send_row_bands(out, 1, si1, si2)


def second_forward_kernel(
    last_row, last_col, frames, ri2, rr1, rr2, ri1, total, sums, probe, weights, tables,
    image, projected, all_sums, ext, patch, stage,
):
    last = ext.shape[1] - 1
    n = ext.shape[2]
    ext[...] = total[...]
    add_col_bands(ext, 0, rr1, rr2)
    add_row_bands(ext, 1, ri1, ri2)

    @pl.when(lax.axis_index("wide") == 0)
    def _():
        ext[:, :, :HALO] = jnp.zeros((2, last + 1, HALO, 128), F32)

    @pl.when(lax.axis_index("wide") == last_row)
    def _():
        ext[:, :, n - HALO :] = jnp.zeros((2, last + 1, HALO, 128), F32)

    low = lanes_low((2, n, 128))

    @pl.when(lax.axis_index("narrow") == 0)
    def _():
        ext[:, last] = jnp.where(low, ext[:, last], 0.0)

    @pl.when(lax.axis_index("narrow") == last_col)
    def _():
        ext[:, last] = jnp.where(low, 0.0, ext[:, last])

    for b in range(last):
        image[:, :, 128 * b : 128 * (b + 1)] = ext[:, b, HALO : n - HALO]

    def visit(k, energy):
        take_patch(ext, frames, k, patch)
        pe, po = project(patch, probe, weights, k, tables, stage)
        projected[k] = cat([pe, po], 1)
        return energy + square_sum(pe) + square_sum(po)

    energy = lax.fori_loop(0, frames[0], visit, F32(0.0))
    rows = lax.broadcasted_iota(jnp.int32, (8, 128), 0)
    all_sums[...] = jnp.where(
        rows == 2, square_sum(image[...]), jnp.where(rows == 3, energy, sums[...])
    )


def second_backward_kernel(begin, end, frames, projected, probe, weights, tables, *rest):
    total, stage = rest[-2:]
    h = projected.shape[2] // 2
    if begin == 0:
        total[...] = jnp.zeros_like(total)

    def visit(k, carried):
        pe, po = (projected[k, :, :h], projected[k, :, h:])
        parts = back_project(pe, po, probe, weights, k, tables, stage)
        put_patch(total, frames, k, parts)
        return carried

    lax.fori_loop(begin, jnp.minimum(end, frames[0]), visit, 0)


def send_margins_kernel(total, first, second):
    n = total.shape[2]
    by_parity(
        "wide",
        lambda: total[:, :, :HALO].reshape(first.shape),
        lambda: total[:, :, n - HALO :].reshape(first.shape),
        store(first),
        store(second),
    )


def fold_rows_kernel(second, first, total, *rest):
    parts, (middle, out_first, out_second, out_sums) = (rest[:-4], rest[-4:])
    blocks, n = middle.shape[1:3]
    last = blocks - 1
    above, below = lower_upper("wide", first[...], second[...])
    middle[...] = total[:, :, HALO : HALO + n]
    middle[:, :, :HALO] += above.reshape(2, blocks, HALO, 128)
    middle[:, :, n - HALO :] += below.reshape(2, blocks, HALO, 128)
    low = lanes_low((n, 128))
    re, im = (middle[0, last], pltpu.roll(middle[1, last], HALO, 1))
    by_parity(
        "narrow",
        lambda: jnp.where(low, im, re),
        lambda: jnp.where(low, re, im),
        store(out_first),
        store(out_second),
    )
    out_sums[...] = total_of(parts)


def finish_kernel(second, first, g, image, middle, *rest):
    parts, (solved_out, left_out, solved, left_over, sent) = (rest[:-5], rest[-5:])
    n, width = g.shape[1:]
    left, right = lower_upper("narrow", first[...], second[...])
    low = lanes_low(right.shape)
    total = total_of(parts)
    n0, s0, uu, s1 = (total[i : i + 1, :1] for i in range(4))
    mu = s0 / n0
    a0 = n0 / (s0 + damping * n0)
    n1 = a0 * a0 * (uu - mu * s0)
    b = n1 / n0
    c1 = a0 * mu + b
    curve = damping * (n1 + b * b * n0) + c1 * c1 * s0 - 2.0 * c1 * a0 * uu + a0 * a0 * s1
    a1 = n1 / curve
    last = width // 128 - 1
    for q in range(2):
        low_part = left if q == 0 else pltpu.roll(left, HALO, 1)
        high_part = right if q == 0 else pltpu.roll(right, HALO, 1)
        for block in range(last + 1):
            cols = slice(128 * block, 128 * (block + 1))
            v = middle[q, block]
            if block == 0:
                v = v + jnp.where(low, low_part, 0.0)
            if block == last:
                v = v + jnp.where(low, 0.0, high_part)
            x, u = (g[q, :, cols], image[q, :, cols])
            d1 = c1 * x - a0 * u
            solved[q, :, cols] = a0 * x + a1 * d1
            left_over[q, :, cols] = a0 * (mu * x - u) - a1 * (damping * d1 + c1 * u - a0 * v)
        for i, (value, to) in enumerate(((solved, solved_out), (left_over, left_out))):
            pltpu.make_async_copy(value.at[q], to.at[q], sent.at[q, i]).start()
    for q in range(2):
        for i, (value, to) in enumerate(((solved, solved_out), (left_over, left_out))):
            pltpu.make_async_copy(value.at[q], to.at[q], sent.at[q, i]).wait()


def total_of(refs):
    total = refs[0][...]
    for ref in refs[1:]:
        total = total + ref[...]
    return total


def add_kernel(*refs):
    refs[-1][...] = total_of(refs[:-1])


def hops(axis, steps):
    size = lax.axis_size(axis)
    masks = list(steps) + [sum(steps)] * (len(steps) > 1)
    return [(axis, [(i, i ^ mask) for i in range(size)]) for mask in masks]


def powers(size):
    found = []
    while 2 ** len(found) < size:
        found.append(2 ** len(found))
    return found


def take_hops(x, wanted):
    return [x] + [lax.ppermute(x, axis, perm) for axis, perm in wanted]


def add_hops(x, rounds):
    for wanted in rounds:
        x = call(add_kernel, [shape(8, 128)], 0, take_hops(x, wanted))[0]
    return x


def shape(*dims):
    return jax.ShapeDtypeStruct(dims, F32)


def call(kernel, outs, smem, args, scratch=(), flops=0, aliases={}, far=(), out_far=False):
    specs = [pl.BlockSpec(memory_space=pltpu.SMEM)] * smem
    specs += [pl.BlockSpec(memory_space=pltpu.VMEM)] * (len(args) - smem)
    for i in far:
        specs[i] = pl.BlockSpec(memory_space=pltpu.HBM)
    args = [
        arg if i < smem else pltpu.with_memory_space_constraint(arg, spec.memory_space)
        for i, (arg, spec) in enumerate(zip(args, specs))
    ]
    moved = sum(a.size * a.dtype.itemsize for a in args)
    moved += sum(math.prod(o.shape) * o.dtype.itemsize for o in outs)
    place = pltpu.HBM if out_far else pltpu.VMEM
    return pl.pallas_call(
        kernel,
        out_shape=[place(o.shape, o.dtype) for o in outs],
        in_specs=specs,
        out_specs=[pl.BlockSpec(memory_space=place)] * len(outs),
        scratch_shapes=list(scratch),
        input_output_aliases=aliases,
        compiler_params=pltpu.CompilerParams(vmem_limit_bytes=20 * MIB),
        cost_estimate=pl.CostEstimate(flops=flops, bytes_accessed=moved, transcendentals=0),
    )(*args)


def prepare(frames, w, probe, tables, g):
    slots, modes, parts, rows, cols = w.shape
    sorter = sorting_tables(cols)
    weights = jax.ShapeDtypeStruct((slots, modes, rows, parts * cols), BF16)
    sort_flops = 8 * modes * rows * cols * rows
    scratch = [pltpu.VMEM(w.shape, BF16), pltpu.SemaphoreType.DMA((slots,))]
    outs = [jax.ShapeDtypeStruct(x.shape, x.dtype) for x in (sorter, probe, tables, g)]
    weights, sorter, probe, tables, g = call(
        prepare_kernel, [weights] + outs, 1, [frames, w, sorter, probe, tables, g],
        scratch + [pltpu.SemaphoreType.DMA((4,))], sort_flops, far=(1, 2, 3, 4, 5),
    )
    if slots > 1:
        weights = call(
            prepare_rest_kernel, [weights], 1, [frames, w, sorter, weights],
            scratch, (slots - 1) * sort_flops, {3: 0}, (1,),
        )[0]
    return (weights, probe, tables, g)


def local(gradient, probe_modes, mode_weights, offsets, counts):
    weights = mode_weights[0, 0]
    slots, modes = weights.shape[:2]
    rows, width = gradient.shape[1:]
    tall, blocks = (rows + 2 * HALO, width // 128 + 1)
    frames = jnp.concatenate([counts.reshape(-1), jnp.swapaxes(offsets, 2, 3).reshape(-1)])
    tables = half_tables(width)
    pass_flops = 8 * 2 * slots * modes * 2 * width * width * width
    extended = pltpu.VMEM((2, blocks, tall, 128), F32)
    patch = pltpu.VMEM((2, rows, width), F32)
    stage = pltpu.VMEM((2, modes, rows, width), BF16)
    whole = shape(2, blocks, tall, 128)

    row_sends = call(
        halo_rows_kernel, [shape(2, HALO, width)] * 2, 0, [gradient],
        [pltpu.SemaphoreType.DMA((2,))], far=(0,),
    )
    row2, row1 = (swap(row_sends[1], "wide", 1), swap(row_sends[0], "wide", 0))
    sorted_weights, probe_modes, tables, gradient = prepare(
        frames, weights, probe_modes, tables, gradient
    )
    col_sends = call(
        halo_cols_kernel, [shape(tall, 128)] * 2, 0, [row2, row1, gradient],
        [pltpu.VMEM((2, blocks, tall, 128), F32)],
    )
    col1, col2 = (swap(x, "narrow", i) for i, x in enumerate(col_sends))

    row_band, col_band = (shape(blocks * 2 * HALO, 128), shape(tall, 128))
    total, sums, sr1, sr2, si1, si2 = call(
        first_pass_kernel,
        [whole, shape(8, 128), row_band, row_band, col_band, col_band],
        1,
        [frames, gradient, row1, row2, col1, col2, probe_modes, sorted_weights, tables],
        [extended, patch, stage],
        pass_flops,
    )
    sr2, si1, si2, sr1 = (
        swap(sr2, "wide", 1), swap(si1, "narrow", 0), swap(si2, "narrow", 1), swap(sr1, "wide", 0)
    )
    total, sr1, sr2, si1, si2 = call(
        bands_kernel,
        [whole, col_band, col_band, row_band, row_band],
        0,
        [sr2, si1, si2, sr1, total],
        aliases={4: 0},
    )
    si2, sr1, sr2, si1 = (
        swap(si2, "wide", 1), swap(sr1, "narrow", 0), swap(sr2, "narrow", 1), swap(si1, "wide", 0)
    )
    image, projected, sums = call(
        functools.partial(
            second_forward_kernel, lax.axis_size("wide") - 1, lax.axis_size("narrow") - 1
        ),
        [shape(2, rows, width), shape(slots, rows, width), shape(8, 128)],
        1,
        [
            frames, si2, sr1, sr2, si1, total, sums, probe_modes, sorted_weights, tables,
        ],
        [extended, patch, stage],
        pass_flops // 2,
    )
    along_wide, along_narrow = (powers(lax.axis_size("wide")), powers(lax.axis_size("narrow")))
    rounds = [hops("wide", [step]) for step in along_wide[:-1]]
    rounds += [hops("narrow", [step]) for step in along_narrow[:-2]]
    beside_rows = hops("narrow", along_narrow[-2:]) if along_narrow else []
    beside_cols = hops("wide", along_wide[-1:]) if along_wide else []
    early = len(rounds)
    total = None
    for i in range(max(early, 1)):
        begin, end = (i * slots // max(early, 1), (i + 1) * slots // max(early, 1))
        if end > begin:
            total = call(
                functools.partial(second_backward_kernel, begin, end),
                [whole],
                1,
                [frames, projected, probe_modes, sorted_weights, tables]
                + ([] if begin == 0 else [total]),
                [stage],
                pass_flops // 2 * (end - begin) // slots,
                {} if begin == 0 else {5: 0},
            )[0]
        sums = add_hops(sums, rounds[i : i + 1])
        if end > 0:
            total, sums = lax.optimization_barrier((total, sums))
    margin = shape(2 * blocks * HALO, 128)
    f1, f2 = call(send_margins_kernel, [margin, margin], 0, [total])
    f2, f1 = (swap(f2, "wide", 1), swap(f1, "wide", 0))
    middle, f1, f2, sums = call(
        fold_rows_kernel,
        [shape(2, blocks, rows, 128), shape(rows, 128), shape(rows, 128), shape(8, 128)],
        0,
        [f2, f1, total] + take_hops(sums, beside_rows),
    )
    f2, f1 = (swap(f2, "narrow", 1), swap(f1, "narrow", 0))
    solved, left_over = call(
        finish_kernel,
        [shape(2, rows, width)] * 2,
        0,
        [f2, f1, gradient, image, middle] + take_hops(sums, beside_cols),
        [pltpu.VMEM((2, rows, width), F32)] * 2 + [pltpu.SemaphoreType.DMA((2, 2))],
        out_far=True,
    )
    return (solved, left_over)


def solution(mesh):
    placed = (
        P(None, "wide", "narrow"),
        P(),
        P("wide", "narrow", None, None, None, None, None),
        P("wide", "narrow", None, None),
        P("wide", "narrow"),
    )
    return jax.shard_map(
        local,
        mesh=mesh,
        in_specs=placed,
        out_specs=(P(None, "wide", "narrow"), P(None, "wide", "narrow")),
        check_vma=False,
    )
```

```python
import functools
import math

import jax
import jax.numpy as jnp
import numpy as np
from jax import lax
from jax.experimental import pallas as pl
from jax.experimental.pallas import tpu as pltpu
from jax.sharding import PartitionSpec as P

HALO = 64
damping = 0.5
F32 = jnp.float32
BF16 = jnp.bfloat16
MIB = 1024 * 1024


def pairs(size, odd):
    found = []
    for i in range(odd, size - 1, 2):
        found += [(i, i + 1), (i + 1, i)]
    return found


def swap(x, axis, odd):
    wanted = pairs(lax.axis_size(axis), odd)
    if not wanted:
        return jnp.zeros_like(x)
    return lax.ppermute(x, axis, wanted)


def half_tables(length):
    counter = np.arange(length)
    angles = ((counter[:, None] * counter[None, :]) % length).astype(np.float32)
    angles = angles * np.float32(2.0 * math.pi / length)
    factor = np.float32(1.0 / math.sqrt(length))
    cos, sin = (np.cos(angles) * factor, np.sin(angles) * factor)
    half = length // 2
    tables = []
    for parity in (0, 1):
        c, s = (cos[parity::2, :half], sin[parity::2, :half])
        left = np.concatenate([np.concatenate([c, s], 1), np.concatenate([-s, c], 1)], 0)
        tables += [left, left.T]
    return jnp.asarray(np.stack(tables), BF16)


def sorting_tables(length):
    order = np.concatenate([np.arange(0, length, 2), np.arange(1, length, 2)])
    left = np.zeros((length, length), np.float32)
    left[np.arange(length), order] = 1.0
    return jnp.asarray(np.stack([left, left.T]), BF16)


def dot(a, b):
    return jnp.dot(a, b, preferred_element_type=F32)


def cat(parts, axis):
    return jnp.concatenate(parts, axis=axis)


def lanes_low(shape):
    return lax.broadcasted_iota(jnp.int32, shape, len(shape) - 1) < shape[-1] // 2


def shifted_place(frames, k, blocks):
    row = HALO + frames[1][0, k]
    col = frames[1][1, k]
    first = jnp.where(col < 0, blocks - 1, 0)
    places = [lax.rem(first + i, blocks) for i in range(blocks)]
    return (row, places, jnp.where(col < 0, col + 128, col))


def take_patch(ext, frames, k, patch):
    width = patch.shape[1]
    row, places, across = shifted_place(frames, k, ext.shape[1])
    lane = lax.broadcasted_iota(jnp.int32, (width, 128), 1)
    back = lax.rem(128 - across, 128)
    for q in range(2):
        found = [ext[q, place, pl.ds(row, width), :] for place in places]
        for i in range(width // 128):
            both = jnp.where(lane >= across, found[i], found[i + 1])
            patch[q, :, 128 * i : 128 * (i + 1)] = pltpu.roll(both, back, 1)


def put_patch(total, frames, k, parts):
    width = parts[0].shape[0]
    row, places, across = shifted_place(frames, k, total.shape[1])
    lane = lax.broadcasted_iota(jnp.int32, (width, 128), 1)
    none = jnp.zeros((width, 128), F32)
    for q in range(2):
        turned = [none]
        for i in range(width // 128):
            turned.append(pltpu.roll(parts[q][:, 128 * i : 128 * (i + 1)], across, 1))
        turned.append(none)
        for i, place in enumerate(places):
            total[q, place, pl.ds(row, width), :] += jnp.where(
                lane < across, turned[i], turned[i + 1]
            )


def project(patch, probe, weights, k, tables, stage):
    te, te_t, to, to_t = (tables[i] for i in range(4))
    xr, xi = (patch[0], patch[1])
    width = xr.shape[0]
    h = width // 2
    modes = probe.shape[0]
    for m in range(modes):
        pr, pi = (probe[m, 0].astype(F32), probe[m, 1].astype(F32))
        er, ei = (pr * xr - pi * xi, pr * xi + pi * xr)
        even = cat([er[:h] + er[h:], ei[:h] + ei[h:]], 0).astype(BF16)
        odd = cat([er[:h] - er[h:], ei[:h] - ei[h:]], 0).astype(BF16)
        for e, y in enumerate((dot(te, even), dot(to, odd))):
            yr, yi = (y[:h], y[h:])
            plus = cat([yr[:, :h] + yr[:, h:], yi[:, :h] + yi[:, h:]], 1)
            minus = cat([yr[:, :h] - yr[:, h:], yi[:, :h] - yi[:, h:]], 1)
            stage[0, m, e * h : (e + 1) * h] = plus.astype(BF16)
            stage[1, m, e * h : (e + 1) * h] = minus.astype(BF16)
    found = []
    for e, table in enumerate((te_t, to_t)):
        acc = None
        for m in range(modes):
            z = dot(stage[e, m], table)
            z = z * weights[k, m, :, e * width : (e + 1) * width].astype(F32)
            acc = z if m == 0 else acc + z
        found.append(acc[:, :h] + acc[:, h:])
    return tuple(found)


def back_project(pe, po, probe, weights, k, tables, stage):
    te, te_t, to, to_t = (tables[i] for i in range(4))
    width = pe.shape[0]
    h = width // 2
    modes = probe.shape[0]
    pe2, po2 = (cat([pe, pe], 1), cat([po, po], 1))
    for m in range(modes):
        ve = (weights[k, m, :, :width].astype(F32) * pe2).astype(BF16)
        vo = (weights[k, m, :, width:].astype(F32) * po2).astype(BF16)
        top = cat([cat([ve[:h, :h], vo[:h, :h]], 1), cat([ve[:h, h:], vo[:h, h:]], 1)], 0)
        low = cat([cat([ve[h:, :h], vo[h:, :h]], 1), cat([ve[h:, h:], vo[h:, h:]], 1)], 0)
        a, b = (dot(te_t, top), dot(to_t, low))
        s, d = (a + b, a - b)
        for e, c in enumerate((slice(0, h), slice(h, width))):
            stage[e, m, :h] = cat([s[:h, c], s[h:, c]], 1).astype(BF16)
            stage[e, m, h:] = cat([d[:h, c], d[h:, c]], 1).astype(BF16)
    cr = ci = None
    for m in range(modes):
        a, b = (dot(stage[0, m], te), dot(stage[1, m], to))
        s, d = (a + b, a - b)
        nr, ni = (cat([s[:, :h], d[:, :h]], 1), cat([s[:, h:], d[:, h:]], 1))
        pr, pi = (probe[m, 0].astype(F32), probe[m, 1].astype(F32))
        r = pr * nr + pi * ni
        i = pr * ni - pi * nr
        cr = r if m == 0 else cr + r
        ci = i if m == 0 else ci + i
    return (cr, ci)


def square_sum(x):
    return jnp.sum(x * x)


def scalar_tile(values):
    rows = lax.broadcasted_iota(jnp.int32, (8, 128), 0)
    tile = jnp.zeros((8, 128), F32)
    for i, value in enumerate(values):
        tile = jnp.where(rows == i, value, tile)
    return tile


def parity_of(axis):
    return lax.rem(lax.axis_index(axis), 2)


def by_parity(axis, low, high, first, second):
    even = parity_of(axis) == 0

    @pl.when(even)
    def _():
        first(high())
        second(low())

    @pl.when(jnp.logical_not(even))
    def _():
        first(low())
        second(high())


def lower_upper(axis, first, second):
    even = parity_of(axis) == 0
    return (jnp.where(even, second, first), jnp.where(even, first, second))


def store(ref):
    def put(value):
        ref[...] = value

    return put


def halo_kernel(g, row1, row2, col1, col2, ends, arrived):
    n, width = g.shape[1:]

    def move(source, to, i):
        return pltpu.make_async_copy(source, to, arrived.at[i])

    sides = [move(g.at[:, :, at : at + 128], ends.at[i], i) for i, at in enumerate((0, width - 128))]
    for side in sides:
        side.start()
    low, high = (g.at[:, :HALO], g.at[:, n - HALO :])
    by_parity(
        "wide",
        lambda: low,
        lambda: high,
        lambda source: move(source, row1, 2).start(),
        lambda source: move(source, row2, 3).start(),
    )
    for side in sides:
        side.wait()
    half = lanes_low(col1.shape)
    by_parity(
        "narrow",
        lambda: jnp.where(half, ends[0, 0], pltpu.roll(ends[0, 1], HALO, 1)),
        lambda: jnp.where(half, pltpu.roll(ends[1, 1], HALO, 1), ends[1, 0]),
        store(col1),
        store(col2),
    )
    move(low, row1, 2).wait()
    move(low, row2, 3).wait()


def fill_cols(put, first, second):
    left, right = lower_upper("narrow", first[...], second[...])
    low = lanes_low(right.shape)
    put(0, jnp.where(low, right, left))
    put(1, pltpu.roll(jnp.where(low, left, right), HALO, 1))


def corners_kernel(col2, col1, first, second, beside):
    n = beside.shape[1]

    def put(q, value):
        beside[q] = value

    fill_cols(put, col1, col2)
    by_parity(
        "wide",
        lambda: beside[:, :HALO],
        lambda: beside[:, n - HALO :],
        store(first),
        store(second),
    )


def fill_tile(ext, g, row1, row2, col1, col2, corner1, corner2):
    n, width = g.shape[1:]
    last = width // 128
    above, below = lower_upper("wide", row1[...], row2[...])
    for b in range(last):
        cols = slice(128 * b, 128 * (b + 1))
        ext[:, b, :HALO] = above[:, :, cols]
        ext[:, b, HALO : HALO + n] = g[:, :, cols]
        ext[:, b, HALO + n :] = below[:, :, cols]

    def put(q, value):
        ext[q, last, HALO : HALO + n] = value

    fill_cols(put, col1, col2)
    above, below = lower_upper("wide", corner1[...], corner2[...])
    ext[:, last, :HALO] = above
    ext[:, last, HALO + n :] = below


def sort_weights(frames, w, sorter, out, held, arrived, begin, end, meanwhile):
    width = w.shape[-1]
    h = width // 2
    modes = w.shape[1]

    def fetch(k):
        return pltpu.make_async_copy(w.at[k], held.at[k], arrived.at[k])

    for k in range(begin, end):

        @pl.when(k < frames[0][0])
        def _():
            fetch(k).start()

    meanwhile()

    def visit(k, carried):
        fetch(k).wait()
        for m in range(modes):
            re = dot(dot(sorter[0], held[k, m, 0]).astype(BF16), sorter[1])
            im = dot(dot(sorter[0], held[k, m, 1]).astype(BF16), sorter[1])
            out[k, m] = cat([re[:, :h], im[:, :h], re[:, h:], im[:, h:]], 1).astype(BF16)
        return carried

    lax.fori_loop(begin, jnp.minimum(end, frames[0][0]), visit, 0)


def prepare_kernel(
    counts, corner, w, sorter_far, probe_far, tables_far, g_far,
    out, probe, tables, g, held, sorter, arrived, loaded,
):
    frames = (counts, None)
    moves = ((sorter_far, sorter), (g_far, g), (probe_far, probe), (tables_far, tables))
    moves = [pltpu.make_async_copy(a, b, loaded.at[i]) for i, (a, b) in enumerate(moves)]
    moves[0].start()

    def meanwhile():
        for move in moves[1:]:
            move.start()
        moves[0].wait()

    sort_weights(frames, w, sorter, out, held, arrived, 0, w.shape[0], meanwhile)
    for move in moves[1:]:
        move.wait()


def first_pass_kernel(
    counts, offsets, row2, row1, g, col1, col2, corner1, corner2, probe, weights, tables,
    total, sums, sr1, sr2, si1, si2, ext, patch, stage,
):
    frames = (counts, offsets)
    fill_tile(ext, g, row1, row2, col1, col2, corner1, corner2)
    total[...] = jnp.zeros_like(total)

    def visit(k, energy):
        take_patch(ext, frames, k, patch)
        pe, po = project(patch, probe, weights, k, tables, stage)
        put_patch(total, frames, k, back_project(pe, po, probe, weights, k, tables, stage))
        return energy + square_sum(pe) + square_sum(po)

    energy = lax.fori_loop(0, frames[0][0], visit, F32(0.0))
    sums[...] = scalar_tile([square_sum(g[...]), energy])
    send_row_bands(total, 0, sr1, sr2)
    send_col_bands(total, 1, si1, si2)


def send_row_bands(total, q, first, second):
    n = total.shape[2]
    by_parity(
        "wide",
        lambda: total[q, :, : 2 * HALO].reshape(first.shape),
        lambda: total[q, :, n - 2 * HALO :].reshape(first.shape),
        store(first),
        store(second),
    )


def send_col_bands(total, q, first, second):
    last = total.shape[1] - 1
    low = lanes_low(first.shape)
    by_parity(
        "narrow",
        lambda: jnp.where(low, total[q, 0], total[q, last]),
        lambda: jnp.where(low, total[q, last], total[q, last - 1]),
        store(first),
        store(second),
    )


def add_row_bands(total, q, first, second):
    blocks, n = total.shape[1:3]
    above, below = lower_upper("wide", first[...], second[...])
    total[q, :, : 2 * HALO] += above.reshape(blocks, 2 * HALO, 128)
    total[q, :, n - 2 * HALO :] += below.reshape(blocks, 2 * HALO, 128)


def add_col_bands(total, q, first, second):
    last = total.shape[1] - 1
    left, right = lower_upper("narrow", first[...], second[...])
    low = lanes_low(right.shape)
    total[q, last] += jnp.where(low, right, left)
    total[q, 0] += jnp.where(low, left, 0.0)
    total[q, last - 1] += jnp.where(low, 0.0, right)


def bands_kernel(rr2, ri1, ri2, rr1, total, out, sr1, sr2, si1, si2):
    add_row_bands(out, 0, rr1, rr2)
    add_col_bands(out, 1, ri1, ri2)
    send_col_bands(out, 0, sr1, sr2)
    send_row_bands(out, 1, si1, si2)


def second_forward_kernel(
    last_row, last_col, counts, offsets, ri2, rr1, rr2, ri1, total, sums, probe, weights, tables,
    image, projected, all_sums, ext, patch, stage,
):
    frames = (counts, offsets)
    last = ext.shape[1] - 1
    n = ext.shape[2]
    ext[...] = total[...]
    add_col_bands(ext, 0, rr1, rr2)
    add_row_bands(ext, 1, ri1, ri2)

    @pl.when(lax.axis_index("wide") == 0)
    def _():
        ext[:, :, :HALO] = jnp.zeros((2, last + 1, HALO, 128), F32)

    @pl.when(lax.axis_index("wide") == last_row)
    def _():
        ext[:, :, n - HALO :] = jnp.zeros((2, last + 1, HALO, 128), F32)

    low = lanes_low((2, n, 128))

    @pl.when(lax.axis_index("narrow") == 0)
    def _():
        ext[:, last] = jnp.where(low, ext[:, last], 0.0)

    @pl.when(lax.axis_index("narrow") == last_col)
    def _():
        ext[:, last] = jnp.where(low, 0.0, ext[:, last])

    for b in range(last):
        image[:, :, 128 * b : 128 * (b + 1)] = ext[:, b, HALO : n - HALO]

    def visit(k, energy):
        take_patch(ext, frames, k, patch)
        pe, po = project(patch, probe, weights, k, tables, stage)
        projected[k] = cat([pe, po], 1)
        return energy + square_sum(pe) + square_sum(po)

    energy = lax.fori_loop(0, frames[0][0], visit, F32(0.0))
    rows = lax.broadcasted_iota(jnp.int32, (8, 128), 0)
    all_sums[...] = jnp.where(
        rows == 2, square_sum(image[...]), jnp.where(rows == 3, energy, sums[...])
    )


def second_backward_kernel(begin, end, counts, offsets, projected, probe, weights, tables, *rest):
    frames = (counts, offsets)
    total, stage = rest[-2:]
    h = projected.shape[2] // 2
    if begin == 0:
        total[...] = jnp.zeros_like(total)

    def visit(k, carried):
        pe, po = (projected[k, :, :h], projected[k, :, h:])
        parts = back_project(pe, po, probe, weights, k, tables, stage)
        put_patch(total, frames, k, parts)
        return carried

    lax.fori_loop(begin, jnp.minimum(end, frames[0][0]), visit, 0)


def send_margins_kernel(total, first, second):
    n = total.shape[2]
    by_parity(
        "wide",
        lambda: total[:, :, :HALO].reshape(first.shape),
        lambda: total[:, :, n - HALO :].reshape(first.shape),
        store(first),
        store(second),
    )


def fold_rows_kernel(second, first, total, *rest):
    parts, (middle, out_first, out_second, out_sums) = (rest[:-4], rest[-4:])
    blocks, n = middle.shape[1:3]
    last = blocks - 1
    above, below = lower_upper("wide", first[...], second[...])
    middle[...] = total[:, :, HALO : HALO + n]
    middle[:, :, :HALO] += above.reshape(2, blocks, HALO, 128)
    middle[:, :, n - HALO :] += below.reshape(2, blocks, HALO, 128)
    low = lanes_low((n, 128))
    re, im = (middle[0, last], pltpu.roll(middle[1, last], HALO, 1))
    by_parity(
        "narrow",
        lambda: jnp.where(low, im, re),
        lambda: jnp.where(low, re, im),
        store(out_first),
        store(out_second),
    )
    out_sums[...] = total_of(parts)


def finish_kernel(second, first, g, image, middle, *rest):
    parts, (solved_out, left_out, solved, left_over, sent) = (rest[:-5], rest[-5:])
    n, width = g.shape[1:]
    left, right = lower_upper("narrow", first[...], second[...])
    low = lanes_low(right.shape)
    total = total_of(parts)
    n0, s0, uu, s1 = (total[i : i + 1, :1] for i in range(4))
    mu = s0 / n0
    a0 = n0 / (s0 + damping * n0)
    n1 = a0 * a0 * (uu - mu * s0)
    b = n1 / n0
    c1 = a0 * mu + b
    curve = damping * (n1 + b * b * n0) + c1 * c1 * s0 - 2.0 * c1 * a0 * uu + a0 * a0 * s1
    a1 = n1 / curve
    last = width // 128 - 1
    for q in range(2):
        low_part = left if q == 0 else pltpu.roll(left, HALO, 1)
        high_part = right if q == 0 else pltpu.roll(right, HALO, 1)
        for block in range(last + 1):
            cols = slice(128 * block, 128 * (block + 1))
            v = middle[q, block]
            if block == 0:
                v = v + jnp.where(low, low_part, 0.0)
            if block == last:
                v = v + jnp.where(low, 0.0, high_part)
            x, u = (g[q, :, cols], image[q, :, cols])
            d1 = c1 * x - a0 * u
            solved[q, :, cols] = a0 * x + a1 * d1
            left_over[q, :, cols] = a0 * (mu * x - u) - a1 * (damping * d1 + c1 * u - a0 * v)
        for i, (value, to) in enumerate(((solved, solved_out), (left_over, left_out))):
            pltpu.make_async_copy(value.at[q], to.at[q], sent.at[q, i]).start()
    for q in range(2):
        for i, (value, to) in enumerate(((solved, solved_out), (left_over, left_out))):
            pltpu.make_async_copy(value.at[q], to.at[q], sent.at[q, i]).wait()


def total_of(refs):
    total = refs[0][...]
    for ref in refs[1:]:
        total = total + ref[...]
    return total


def add_kernel(*refs):
    refs[-1][...] = total_of(refs[:-1])


def hops(axis, steps):
    size = lax.axis_size(axis)
    masks = list(steps) + [sum(steps)] * (len(steps) > 1)
    return [(axis, [(i, i ^ mask) for i in range(size)]) for mask in masks]


def powers(size):
    found = []
    while 2 ** len(found) < size:
        found.append(2 ** len(found))
    return found


def take_hops(x, wanted):
    return [x] + [lax.ppermute(x, axis, perm) for axis, perm in wanted]


def add_hops(x, rounds):
    for wanted in rounds:
        x = call(add_kernel, [shape(8, 128)], 0, take_hops(x, wanted))[0]
    return x


def shape(*dims):
    return jax.ShapeDtypeStruct(dims, F32)


def call(kernel, outs, smem, args, scratch=(), flops=0, aliases={}, far=(), out_far=False):
    specs = [pl.BlockSpec(memory_space=pltpu.SMEM)] * smem
    specs += [pl.BlockSpec(memory_space=pltpu.VMEM)] * (len(args) - smem)
    for i in far:
        specs[i] = pl.BlockSpec(memory_space=pltpu.HBM)
    args = [
        arg if i < smem else pltpu.with_memory_space_constraint(arg, spec.memory_space)
        for i, (arg, spec) in enumerate(zip(args, specs))
    ]
    moved = sum(a.size * a.dtype.itemsize for a in args)
    moved += sum(math.prod(o.shape) * o.dtype.itemsize for o in outs)
    place = pltpu.HBM if out_far else pltpu.VMEM
    return pl.pallas_call(
        kernel,
        out_shape=[place(o.shape, o.dtype) for o in outs],
        in_specs=specs,
        out_specs=[pl.BlockSpec(memory_space=place)] * len(outs),
        scratch_shapes=list(scratch),
        input_output_aliases=aliases,
        compiler_params=pltpu.CompilerParams(vmem_limit_bytes=20 * MIB),
        cost_estimate=pl.CostEstimate(flops=flops, bytes_accessed=moved, transcendentals=0),
    )(*args)


def prepare(counts, corner, w, probe, tables, g):
    slots, modes, parts, rows, cols = w.shape
    sorter = sorting_tables(cols)
    weights = jax.ShapeDtypeStruct((slots, modes, rows, parts * cols), BF16)
    outs = [jax.ShapeDtypeStruct(x.shape, x.dtype) for x in (probe, tables, g)]
    scratch = [pltpu.VMEM(x.shape, BF16) for x in (w, sorter)]
    scratch += [pltpu.SemaphoreType.DMA((slots,)), pltpu.SemaphoreType.DMA((4,))]
    return call(
        prepare_kernel, [weights] + outs, 1, [counts, corner, w, sorter, probe, tables, g],
        scratch, 8 * slots * modes * rows * cols * rows, far=(2, 3, 4, 5, 6),
    )


def local(gradient, probe_modes, mode_weights, offsets, counts):
    weights = mode_weights[0, 0]
    slots, modes = weights.shape[:2]
    rows, width = gradient.shape[1:]
    tall, blocks = (rows + 2 * HALO, width // 128 + 1)
    counts = counts.reshape(-1)
    offsets = jnp.swapaxes(offsets, 2, 3).reshape(offsets.shape[3], offsets.shape[2])
    tables = half_tables(width)
    pass_flops = 8 * 2 * slots * modes * 2 * width * width * width
    extended = pltpu.VMEM((2, blocks, tall, 128), F32)
    patch = pltpu.VMEM((2, rows, width), F32)
    stage = pltpu.VMEM((2, modes, rows, width), BF16)
    whole = shape(2, blocks, tall, 128)

    row_strip, col_strip, corner = (shape(2, HALO, width), shape(rows, 128), shape(2, HALO, 128))
    row1, row2, col1, col2 = call(
        halo_kernel, [row_strip, row_strip, col_strip, col_strip], 0, [gradient],
        [pltpu.VMEM((2, 2, rows, 128), F32), pltpu.SemaphoreType.DMA((4,))], far=(0,),
    )
    col1, col2 = (swap(col1, "narrow", 0), swap(col2, "narrow", 1))
    row2, row1 = (swap(row2, "wide", 1), swap(row1, "wide", 0))
    corner1, corner2 = call(
        corners_kernel, [corner, corner], 0, [col2, col1], [pltpu.VMEM((2, rows, 128), F32)]
    )
    sorted_weights, probe_modes, tables, gradient = prepare(
        counts, corner1, weights, probe_modes, tables, gradient
    )
    corner2, corner1 = (swap(corner2, "wide", 1), swap(corner1, "wide", 0))

    row_band, col_band = (shape(blocks * 2 * HALO, 128), shape(tall, 128))
    total, sums, sr1, sr2, si1, si2 = call(
        first_pass_kernel,
        [whole, shape(8, 128), row_band, row_band, col_band, col_band],
        2,
        [
            counts, offsets, row2, row1, gradient, col1, col2, corner1, corner2,
            probe_modes, sorted_weights, tables,
        ],
        [extended, patch, stage],
        pass_flops,
    )
    sr2, si1, si2, sr1 = (
        swap(sr2, "wide", 1), swap(si1, "narrow", 0), swap(si2, "narrow", 1), swap(sr1, "wide", 0)
    )
    total, sr1, sr2, si1, si2 = call(
        bands_kernel,
        [whole, col_band, col_band, row_band, row_band],
        0,
        [sr2, si1, si2, sr1, total],
        aliases={4: 0},
    )
    si2, sr1, sr2, si1 = (
        swap(si2, "wide", 1), swap(sr1, "narrow", 0), swap(sr2, "narrow", 1), swap(si1, "wide", 0)
    )
    image, projected, sums = call(
        functools.partial(
            second_forward_kernel, lax.axis_size("wide") - 1, lax.axis_size("narrow") - 1
        ),
        [shape(2, rows, width), shape(slots, rows, width), shape(8, 128)],
        2,
        [
            counts, offsets, si2, sr1, sr2, si1, total, sums, probe_modes, sorted_weights, tables,
        ],
        [extended, patch, stage],
        pass_flops // 2,
    )
    along_wide, along_narrow = (powers(lax.axis_size("wide")), powers(lax.axis_size("narrow")))
    rounds = [hops("wide", [step]) for step in along_wide[:-1]]
    rounds += [hops("narrow", [step]) for step in along_narrow[:-2]]
    beside_rows = hops("narrow", along_narrow[-2:]) if along_narrow else []
    beside_cols = hops("wide", along_wide[-1:]) if along_wide else []
    early = len(rounds)
    total = None
    for i in range(max(early, 1)):
        begin, end = (i * slots // max(early, 1), (i + 1) * slots // max(early, 1))
        if end > begin:
            total = call(
                functools.partial(second_backward_kernel, begin, end),
                [whole],
                2,
                [counts, offsets, projected, probe_modes, sorted_weights, tables]
                + ([] if begin == 0 else [total]),
                [stage],
                pass_flops // 2 * (end - begin) // slots,
                {} if begin == 0 else {6: 0},
            )[0]
        sums = add_hops(sums, rounds[i : i + 1])
        if end > 0:
            total, sums = lax.optimization_barrier((total, sums))
    margin = shape(2 * blocks * HALO, 128)
    f1, f2 = call(send_margins_kernel, [margin, margin], 0, [total])
    f2, f1 = (swap(f2, "wide", 1), swap(f1, "wide", 0))
    middle, f1, f2, sums = call(
        fold_rows_kernel,
        [shape(2, blocks, rows, 128), shape(rows, 128), shape(rows, 128), shape(8, 128)],
        0,
        [f2, f1, total] + take_hops(sums, beside_rows),
    )
    f2, f1 = (swap(f2, "narrow", 1), swap(f1, "narrow", 0))
    solved, left_over = call(
        finish_kernel,
        [shape(2, rows, width)] * 2,
        0,
        [f2, f1, gradient, image, middle] + take_hops(sums, beside_cols),
        [pltpu.VMEM((2, rows, width), F32)] * 2 + [pltpu.SemaphoreType.DMA((2, 2))],
        out_far=True,
    )
    return (solved, left_over)


def solution(mesh):
    placed = (
        P(None, "wide", "narrow"),
        P(),
        P("wide", "narrow", None, None, None, None, None),
        P("wide", "narrow", None, None),
        P("wide", "narrow"),
    )
    return jax.shard_map(
        local,
        mesh=mesh,
        in_specs=placed,
        out_specs=(P(None, "wide", "narrow"), P(None, "wide", "narrow")),
        check_vma=False,
    )
```

```python
import functools
import math

import jax
import jax.numpy as jnp
import numpy as np
from jax import lax
from jax.experimental import pallas as pl
from jax.experimental.pallas import tpu as pltpu
from jax.sharding import PartitionSpec as P

HALO = 64
damping = 0.5
F32 = jnp.float32
BF16 = jnp.bfloat16
MIB = 1024 * 1024


def pairs(size, odd):
    found = []
    for i in range(odd, size - 1, 2):
        found += [(i, i + 1), (i + 1, i)]
    return found


def swap(x, axis, odd):
    wanted = pairs(lax.axis_size(axis), odd)
    if not wanted:
        return jnp.zeros_like(x)
    return lax.ppermute(x, axis, wanted)


def half_tables(length):
    counter = np.arange(length)
    angles = ((counter[:, None] * counter[None, :]) % length).astype(np.float32)
    angles = angles * np.float32(2.0 * math.pi / length)
    factor = np.float32(1.0 / math.sqrt(length))
    cos, sin = (np.cos(angles) * factor, np.sin(angles) * factor)
    half = length // 2
    tables = []
    for parity in (0, 1):
        c, s = (cos[parity::2, :half], sin[parity::2, :half])
        left = np.concatenate([np.concatenate([c, s], 1), np.concatenate([-s, c], 1)], 0)
        tables += [left, left.T]
    return jnp.asarray(np.stack(tables), BF16)


def sorting_tables(length):
    order = np.concatenate([np.arange(0, length, 2), np.arange(1, length, 2)])
    left = np.zeros((length, length), np.float32)
    left[np.arange(length), order] = 1.0
    return jnp.asarray(np.stack([left, left.T]), BF16)


def dot(a, b):
    return jnp.dot(a, b, preferred_element_type=F32)


def cat(parts, axis):
    return jnp.concatenate(parts, axis=axis)


def lanes_low(shape):
    return lax.broadcasted_iota(jnp.int32, shape, len(shape) - 1) < shape[-1] // 2


def shifted_place(frames, k, blocks):
    row = HALO + frames[1][0, k]
    col = frames[1][1, k]
    first = jnp.where(col < 0, blocks - 1, 0)
    places = [lax.rem(first + i, blocks) for i in range(blocks)]
    return (row, places, jnp.where(col < 0, col + 128, col))


def take_patch(ext, frames, k, patch):
    width = patch.shape[1]
    row, places, across = shifted_place(frames, k, ext.shape[1])
    lane = lax.broadcasted_iota(jnp.int32, (width, 128), 1)
    back = lax.rem(128 - across, 128)
    for q in range(2):
        found = [ext[q, place, pl.ds(row, width), :] for place in places]
        for i in range(width // 128):
            both = jnp.where(lane >= across, found[i], found[i + 1])
            patch[q, :, 128 * i : 128 * (i + 1)] = pltpu.roll(both, back, 1)


def put_patch(total, frames, k, parts):
    width = parts[0].shape[0]
    row, places, across = shifted_place(frames, k, total.shape[1])
    lane = lax.broadcasted_iota(jnp.int32, (width, 128), 1)
    none = jnp.zeros((width, 128), F32)
    for q in range(2):
        turned = [none]
        for i in range(width // 128):
            turned.append(pltpu.roll(parts[q][:, 128 * i : 128 * (i + 1)], across, 1))
        turned.append(none)
        for i, place in enumerate(places):
            total[q, place, pl.ds(row, width), :] += jnp.where(
                lane < across, turned[i], turned[i + 1]
            )


def project(patch, probe, weights, k, tables, stage):
    te, te_t, to, to_t = (tables[i] for i in range(4))
    xr, xi = (patch[0], patch[1])
    width = xr.shape[0]
    h = width // 2
    modes = probe.shape[0]
    for m in range(modes):
        pr, pi = (probe[m, 0].astype(F32), probe[m, 1].astype(F32))
        er, ei = (pr * xr - pi * xi, pr * xi + pi * xr)
        even = cat([er[:h] + er[h:], ei[:h] + ei[h:]], 0).astype(BF16)
        odd = cat([er[:h] - er[h:], ei[:h] - ei[h:]], 0).astype(BF16)
        for e, y in enumerate((dot(te, even), dot(to, odd))):
            yr, yi = (y[:h], y[h:])
            plus = cat([yr[:, :h] + yr[:, h:], yi[:, :h] + yi[:, h:]], 1)
            minus = cat([yr[:, :h] - yr[:, h:], yi[:, :h] - yi[:, h:]], 1)
            stage[0, m, e * h : (e + 1) * h] = plus.astype(BF16)
            stage[1, m, e * h : (e + 1) * h] = minus.astype(BF16)
    found = []
    for e, table in enumerate((te_t, to_t)):
        acc = None
        for m in range(modes):
            z = dot(stage[e, m], table)
            z = z * weights[k, m, :, e * width : (e + 1) * width].astype(F32)
            acc = z if m == 0 else acc + z
        found.append(acc[:, :h] + acc[:, h:])
    return tuple(found)


def back_project(pe, po, probe, weights, k, tables, stage):
    te, te_t, to, to_t = (tables[i] for i in range(4))
    width = pe.shape[0]
    h = width // 2
    modes = probe.shape[0]
    pe2, po2 = (cat([pe, pe], 1), cat([po, po], 1))
    for m in range(modes):
        ve = (weights[k, m, :, :width].astype(F32) * pe2).astype(BF16)
        vo = (weights[k, m, :, width:].astype(F32) * po2).astype(BF16)
        top = cat([cat([ve[:h, :h], vo[:h, :h]], 1), cat([ve[:h, h:], vo[:h, h:]], 1)], 0)
        low = cat([cat([ve[h:, :h], vo[h:, :h]], 1), cat([ve[h:, h:], vo[h:, h:]], 1)], 0)
        a, b = (dot(te_t, top), dot(to_t, low))
        s, d = (a + b, a - b)
        for e, c in enumerate((slice(0, h), slice(h, width))):
            stage[e, m, :h] = cat([s[:h, c], s[h:, c]], 1).astype(BF16)
            stage[e, m, h:] = cat([d[:h, c], d[h:, c]], 1).astype(BF16)
    cr = ci = None
    for m in range(modes):
        a, b = (dot(stage[0, m], te), dot(stage[1, m], to))
        s, d = (a + b, a - b)
        nr, ni = (cat([s[:, :h], d[:, :h]], 1), cat([s[:, h:], d[:, h:]], 1))
        pr, pi = (probe[m, 0].astype(F32), probe[m, 1].astype(F32))
        r = pr * nr + pi * ni
        i = pr * ni - pi * nr
        cr = r if m == 0 else cr + r
        ci = i if m == 0 else ci + i
    return (cr, ci)


def square_sum(x):
    return jnp.sum(x * x)


def scalar_tile(values):
    rows = lax.broadcasted_iota(jnp.int32, (8, 128), 0)
    tile = jnp.zeros((8, 128), F32)
    for i, value in enumerate(values):
        tile = jnp.where(rows == i, value, tile)
    return tile


def parity_of(axis):
    return lax.rem(lax.axis_index(axis), 2)


def by_parity(axis, low, high, first, second):
    even = parity_of(axis) == 0

    @pl.when(even)
    def _():
        first(high())
        second(low())

    @pl.when(jnp.logical_not(even))
    def _():
        first(low())
        second(high())


def lower_upper(axis, first, second):
    even = parity_of(axis) == 0
    return (jnp.where(even, second, first), jnp.where(even, first, second))


def store(ref):
    def put(value):
        ref[...] = value

    return put


def halo_kernel(g, row1, row2, col1, col2, ends, arrived):
    n, width = g.shape[1:]

    def move(source, to, i):
        return pltpu.make_async_copy(source, to, arrived.at[i])

    sides = [move(g.at[:, :, at : at + 128], ends.at[i], i) for i, at in enumerate((0, width - 128))]
    for side in sides:
        side.start()
    low, high = (g.at[:, :HALO], g.at[:, n - HALO :])
    by_parity(
        "wide",
        lambda: low,
        lambda: high,
        lambda source: move(source, row1, 2).start(),
        lambda source: move(source, row2, 3).start(),
    )
    for side in sides:
        side.wait()
    half = lanes_low(col1.shape)
    by_parity(
        "narrow",
        lambda: jnp.where(half, ends[0, 0], pltpu.roll(ends[0, 1], HALO, 1)),
        lambda: jnp.where(half, pltpu.roll(ends[1, 1], HALO, 1), ends[1, 0]),
        store(col1),
        store(col2),
    )
    move(low, row1, 2).wait()
    move(low, row2, 3).wait()


def fill_cols(put, first, second):
    left, right = lower_upper("narrow", first[...], second[...])
    low = lanes_low(right.shape)
    put(0, jnp.where(low, right, left))
    put(1, pltpu.roll(jnp.where(low, left, right), HALO, 1))


def corners_kernel(col2, col1, first, second, beside):
    n = beside.shape[1]

    def put(q, value):
        beside[q] = value

    fill_cols(put, col1, col2)
    by_parity(
        "wide",
        lambda: beside[:, :HALO],
        lambda: beside[:, n - HALO :],
        store(first),
        store(second),
    )


def fill_tile(ext, g, row1, row2, col1, col2, corner1, corner2):
    n, width = g.shape[1:]
    last = width // 128
    above, below = lower_upper("wide", row1[...], row2[...])
    for b in range(last):
        cols = slice(128 * b, 128 * (b + 1))
        ext[:, b, :HALO] = above[:, :, cols]
        ext[:, b, HALO : HALO + n] = g[:, :, cols]
        ext[:, b, HALO + n :] = below[:, :, cols]

    def put(q, value):
        ext[q, last, HALO : HALO + n] = value

    fill_cols(put, col1, col2)
    above, below = lower_upper("wide", corner1[...], corner2[...])
    ext[:, last, :HALO] = above
    ext[:, last, HALO + n :] = below


def sort_weights(frames, w, sorter, out, held, arrived, begin, end, meanwhile):
    width = w.shape[-1]
    h = width // 2
    modes = w.shape[1]

    def fetch(k):
        return pltpu.make_async_copy(w.at[k], held.at[k], arrived.at[k])

    for k in range(begin, end):

        @pl.when(k < frames[0][0])
        def _():
            fetch(k).start()

    meanwhile()

    def visit(k, carried):
        fetch(k).wait()
        for m in range(modes):
            re = dot(dot(sorter[0], held[k, m, 0]).astype(BF16), sorter[1])
            im = dot(dot(sorter[0], held[k, m, 1]).astype(BF16), sorter[1])
            out[k, m] = cat([re[:, :h], im[:, :h], re[:, h:], im[:, h:]], 1).astype(BF16)
        return carried

    lax.fori_loop(begin, jnp.minimum(end, frames[0][0]), visit, 0)


def prepare_kernel(
    counts, corner, w, sorter_far, probe_far, tables_far, g_far,
    out, probe, tables, g, held, sorter, arrived, loaded,
):
    frames = (counts, None)
    moves = ((sorter_far, sorter), (g_far, g), (probe_far, probe), (tables_far, tables))
    moves = [pltpu.make_async_copy(a, b, loaded.at[i]) for i, (a, b) in enumerate(moves)]
    moves[0].start()

    def meanwhile():
        for move in moves[1:]:
            move.start()
        moves[0].wait()

    sort_weights(frames, w, sorter, out, held, arrived, 0, w.shape[0], meanwhile)
    for move in moves[1:]:
        move.wait()


def first_pass_kernel(
    counts, offsets, row2, row1, g, col1, col2, corner1, corner2, probe, weights, tables,
    total, sums, sr1, sr2, si1, si2, ext, patch, stage,
):
    frames = (counts, offsets)
    fill_tile(ext, g, row1, row2, col1, col2, corner1, corner2)
    total[...] = jnp.zeros_like(total)

    def visit(k, energy):
        take_patch(ext, frames, k, patch)
        pe, po = project(patch, probe, weights, k, tables, stage)
        put_patch(total, frames, k, back_project(pe, po, probe, weights, k, tables, stage))
        return energy + square_sum(pe) + square_sum(po)

    energy = lax.fori_loop(0, frames[0][0], visit, F32(0.0))
    sums[...] = scalar_tile([square_sum(g[...]), energy])
    send_row_bands(total, 0, sr1, sr2)
    send_col_bands(total, 1, si1, si2)


def send_row_bands(total, q, first, second):
    n = total.shape[2]
    by_parity(
        "wide",
        lambda: total[q, :, : 2 * HALO].reshape(first.shape),
        lambda: total[q, :, n - 2 * HALO :].reshape(first.shape),
        store(first),
        store(second),
    )


def send_col_bands(total, q, first, second):
    last = total.shape[1] - 1
    low = lanes_low(first.shape)
    by_parity(
        "narrow",
        lambda: jnp.where(low, total[q, 0], total[q, last]),
        lambda: jnp.where(low, total[q, last], total[q, last - 1]),
        store(first),
        store(second),
    )


def add_row_bands(total, q, first, second):
    blocks, n = total.shape[1:3]
    above, below = lower_upper("wide", first[...], second[...])
    total[q, :, : 2 * HALO] += above.reshape(blocks, 2 * HALO, 128)
    total[q, :, n - 2 * HALO :] += below.reshape(blocks, 2 * HALO, 128)


def add_col_bands(total, q, first, second):
    last = total.shape[1] - 1
    left, right = lower_upper("narrow", first[...], second[...])
    low = lanes_low(right.shape)
    total[q, last] += jnp.where(low, right, left)
    total[q, 0] += jnp.where(low, left, 0.0)
    total[q, last - 1] += jnp.where(low, 0.0, right)


def bands_kernel(rr2, ri1, ri2, rr1, total, out, sr1, sr2, si1, si2):
    add_row_bands(out, 0, rr1, rr2)
    add_col_bands(out, 1, ri1, ri2)
    send_col_bands(out, 0, sr1, sr2)
    send_row_bands(out, 1, si1, si2)


def second_forward_kernel(
    last_row, last_col, counts, offsets, ri2, rr1, rr2, ri1, total, sums, probe, weights, tables,
    image, projected, all_sums, ext, patch, stage,
):
    frames = (counts, offsets)
    last = ext.shape[1] - 1
    n = ext.shape[2]
    ext[...] = total[...]
    add_col_bands(ext, 0, rr1, rr2)
    add_row_bands(ext, 1, ri1, ri2)

    @pl.when(lax.axis_index("wide") == 0)
    def _():
        ext[:, :, :HALO] = jnp.zeros((2, last + 1, HALO, 128), F32)

    @pl.when(lax.axis_index("wide") == last_row)
    def _():
        ext[:, :, n - HALO :] = jnp.zeros((2, last + 1, HALO, 128), F32)

    low = lanes_low((2, n, 128))

    @pl.when(lax.axis_index("narrow") == 0)
    def _():
        ext[:, last] = jnp.where(low, ext[:, last], 0.0)

    @pl.when(lax.axis_index("narrow") == last_col)
    def _():
        ext[:, last] = jnp.where(low, 0.0, ext[:, last])

    for b in range(last):
        image[:, :, 128 * b : 128 * (b + 1)] = ext[:, b, HALO : n - HALO]

    def visit(k, energy):
        take_patch(ext, frames, k, patch)
        pe, po = project(patch, probe, weights, k, tables, stage)
        projected[k] = cat([pe, po], 1)
        return energy + square_sum(pe) + square_sum(po)

    energy = lax.fori_loop(0, frames[0][0], visit, F32(0.0))
    rows = lax.broadcasted_iota(jnp.int32, (8, 128), 0)
    all_sums[...] = jnp.where(
        rows == 2, square_sum(image[...]), jnp.where(rows == 3, energy, sums[...])
    )


def second_backward_kernel(begin, end, counts, offsets, projected, probe, weights, tables, *rest):
    frames = (counts, offsets)
    total, stage = rest[-2:]
    h = projected.shape[2] // 2
    if begin == 0:
        total[...] = jnp.zeros_like(total)

    def visit(k, carried):
        pe, po = (projected[k, :, :h], projected[k, :, h:])
        parts = back_project(pe, po, probe, weights, k, tables, stage)
        put_patch(total, frames, k, parts)
        return carried

    lax.fori_loop(begin, jnp.minimum(end, frames[0][0]), visit, 0)


def send_margins_kernel(total, first, second):
    n = total.shape[2]
    by_parity(
        "wide",
        lambda: total[:, :, :HALO].reshape(first.shape),
        lambda: total[:, :, n - HALO :].reshape(first.shape),
        store(first),
        store(second),
    )


def fold_rows_kernel(second, first, total, *rest):
    parts, (middle, out_first, out_second, out_sums) = (rest[:-4], rest[-4:])
    blocks, n = middle.shape[1:3]
    last = blocks - 1
    above, below = lower_upper("wide", first[...], second[...])
    middle[...] = total[:, :, HALO : HALO + n]
    middle[:, :, :HALO] += above.reshape(2, blocks, HALO, 128)
    middle[:, :, n - HALO :] += below.reshape(2, blocks, HALO, 128)
    low = lanes_low((n, 128))
    re, im = (middle[0, last], pltpu.roll(middle[1, last], HALO, 1))
    by_parity(
        "narrow",
        lambda: jnp.where(low, im, re),
        lambda: jnp.where(low, re, im),
        store(out_first.at[:n]),
        store(out_second.at[:n]),
    )
    out_first[n:] = total_of(parts)
    out_second[n:] = out_first[n:]
    out_sums[...] = out_first[n:]


def finish_kernel(
    second, first, g, image, middle, sums, solved_out, left_out, solved, left_over, sent
):
    n, width = g.shape[1:]
    left, right = lower_upper("narrow", first[:n], second[:n])
    low = lanes_low(right.shape)
    total = sums[...] + first[n:]
    n0, s0, uu, s1 = (total[i : i + 1, :1] for i in range(4))
    mu = s0 / n0
    a0 = n0 / (s0 + damping * n0)
    n1 = a0 * a0 * (uu - mu * s0)
    b = n1 / n0
    c1 = a0 * mu + b
    curve = damping * (n1 + b * b * n0) + c1 * c1 * s0 - 2.0 * c1 * a0 * uu + a0 * a0 * s1
    a1 = n1 / curve
    last = width // 128 - 1
    for q in range(2):
        low_part = left if q == 0 else pltpu.roll(left, HALO, 1)
        high_part = right if q == 0 else pltpu.roll(right, HALO, 1)
        for block in range(last + 1):
            cols = slice(128 * block, 128 * (block + 1))
            v = middle[q, block]
            if block == 0:
                v = v + jnp.where(low, low_part, 0.0)
            if block == last:
                v = v + jnp.where(low, 0.0, high_part)
            x, u = (g[q, :, cols], image[q, :, cols])
            d1 = c1 * x - a0 * u
            solved[q, :, cols] = a0 * x + a1 * d1
            left_over[q, :, cols] = a0 * (mu * x - u) - a1 * (damping * d1 + c1 * u - a0 * v)
        for i, (value, to) in enumerate(((solved, solved_out), (left_over, left_out))):
            pltpu.make_async_copy(value.at[q], to.at[q], sent.at[q, i]).start()
    for q in range(2):
        for i, (value, to) in enumerate(((solved, solved_out), (left_over, left_out))):
            pltpu.make_async_copy(value.at[q], to.at[q], sent.at[q, i]).wait()


def total_of(refs):
    total = refs[0][...]
    for ref in refs[1:]:
        total = total + ref[...]
    return total


def add_kernel(*refs):
    refs[-1][...] = total_of(refs[:-1])


def hops(over_wide, over_narrow):
    rows, cols = (lax.axis_size("wide"), lax.axis_size("narrow"))
    pairs_of = [(down, right) for down in {0, over_wide} for right in {0, over_narrow}]
    return [
        [
            (i * cols + j, (i ^ down) * cols + (j ^ right))
            for i in range(rows)
            for j in range(cols)
        ]
        for down, right in sorted(pairs_of)
        if down or right
    ]


def powers(size):
    found = []
    while 2 ** len(found) < size:
        found.append(2 ** len(found))
    return found


def take_hops(x, wanted):
    return [x] + [lax.ppermute(x, ("wide", "narrow"), perm) for perm in wanted]


def add_hops(x, rounds):
    for wanted in rounds:
        x = call(add_kernel, [shape(8, 128)], 0, take_hops(x, wanted))[0]
    return x


def shape(*dims):
    return jax.ShapeDtypeStruct(dims, F32)


def call(kernel, outs, smem, args, scratch=(), flops=0, aliases={}, far=(), out_far=False):
    specs = [pl.BlockSpec(memory_space=pltpu.SMEM)] * smem
    specs += [pl.BlockSpec(memory_space=pltpu.VMEM)] * (len(args) - smem)
    for i in far:
        specs[i] = pl.BlockSpec(memory_space=pltpu.HBM)
    args = [
        arg if i < smem else pltpu.with_memory_space_constraint(arg, spec.memory_space)
        for i, (arg, spec) in enumerate(zip(args, specs))
    ]
    moved = sum(a.size * a.dtype.itemsize for a in args)
    moved += sum(math.prod(o.shape) * o.dtype.itemsize for o in outs)
    place = pltpu.HBM if out_far else pltpu.VMEM
    return pl.pallas_call(
        kernel,
        out_shape=[place(o.shape, o.dtype) for o in outs],
        in_specs=specs,
        out_specs=[pl.BlockSpec(memory_space=place)] * len(outs),
        scratch_shapes=list(scratch),
        input_output_aliases=aliases,
        compiler_params=pltpu.CompilerParams(vmem_limit_bytes=20 * MIB),
        cost_estimate=pl.CostEstimate(flops=flops, bytes_accessed=moved, transcendentals=0),
    )(*args)


def prepare(counts, corner, w, probe, tables, g):
    slots, modes, parts, rows, cols = w.shape
    sorter = sorting_tables(cols)
    weights = jax.ShapeDtypeStruct((slots, modes, rows, parts * cols), BF16)
    outs = [jax.ShapeDtypeStruct(x.shape, x.dtype) for x in (probe, tables, g)]
    scratch = [pltpu.VMEM(x.shape, BF16) for x in (w, sorter)]
    scratch += [pltpu.SemaphoreType.DMA((slots,)), pltpu.SemaphoreType.DMA((4,))]
    return call(
        prepare_kernel, [weights] + outs, 1, [counts, corner, w, sorter, probe, tables, g],
        scratch, 8 * slots * modes * rows * cols * rows, far=(2, 3, 4, 5, 6),
    )


def local(gradient, probe_modes, mode_weights, offsets, counts):
    weights = mode_weights[0, 0]
    slots, modes = weights.shape[:2]
    rows, width = gradient.shape[1:]
    tall, blocks = (rows + 2 * HALO, width // 128 + 1)
    counts = counts.reshape(-1)
    offsets = jnp.swapaxes(offsets, 2, 3).reshape(offsets.shape[3], offsets.shape[2])
    tables = half_tables(width)
    pass_flops = 8 * 2 * slots * modes * 2 * width * width * width
    extended = pltpu.VMEM((2, blocks, tall, 128), F32)
    patch = pltpu.VMEM((2, rows, width), F32)
    stage = pltpu.VMEM((2, modes, rows, width), BF16)
    whole = shape(2, blocks, tall, 128)

    row_strip, col_strip, corner = (shape(2, HALO, width), shape(rows, 128), shape(2, HALO, 128))
    row1, row2, col1, col2 = call(
        halo_kernel, [row_strip, row_strip, col_strip, col_strip], 0, [gradient],
        [pltpu.VMEM((2, 2, rows, 128), F32), pltpu.SemaphoreType.DMA((4,))], far=(0,),
    )
    col1, col2 = (swap(col1, "narrow", 0), swap(col2, "narrow", 1))
    row2, row1 = (swap(row2, "wide", 1), swap(row1, "wide", 0))
    corner1, corner2 = call(
        corners_kernel, [corner, corner], 0, [col2, col1], [pltpu.VMEM((2, rows, 128), F32)]
    )
    sorted_weights, probe_modes, tables, gradient = prepare(
        counts, corner1, weights, probe_modes, tables, gradient
    )
    corner2, corner1 = (swap(corner2, "wide", 1), swap(corner1, "wide", 0))

    row_band, col_band = (shape(blocks * 2 * HALO, 128), shape(tall, 128))
    total, sums, sr1, sr2, si1, si2 = call(
        first_pass_kernel,
        [whole, shape(8, 128), row_band, row_band, col_band, col_band],
        2,
        [
            counts, offsets, row2, row1, gradient, col1, col2, corner1, corner2,
            probe_modes, sorted_weights, tables,
        ],
        [extended, patch, stage],
        pass_flops,
    )
    sr2, si1, si2, sr1 = (
        swap(sr2, "wide", 1), swap(si1, "narrow", 0), swap(si2, "narrow", 1), swap(sr1, "wide", 0)
    )
    total, sr1, sr2, si1, si2 = call(
        bands_kernel,
        [whole, col_band, col_band, row_band, row_band],
        0,
        [sr2, si1, si2, sr1, total],
        aliases={4: 0},
    )
    si2, sr1, sr2, si1 = (
        swap(si2, "wide", 1), swap(sr1, "narrow", 0), swap(sr2, "narrow", 1), swap(si1, "wide", 0)
    )
    image, projected, sums = call(
        functools.partial(
            second_forward_kernel, lax.axis_size("wide") - 1, lax.axis_size("narrow") - 1
        ),
        [shape(2, rows, width), shape(slots, rows, width), shape(8, 128)],
        2,
        [
            counts, offsets, si2, sr1, sr2, si1, total, sums, probe_modes, sorted_weights, tables,
        ],
        [extended, patch, stage],
        pass_flops // 2,
    )
    along_wide, along_narrow = (powers(lax.axis_size("wide")), powers(lax.axis_size("narrow")))
    rounds = [hops(step, 0) for step in along_wide[:-1]]
    rounds += [hops(0, step) for step in along_narrow[1:-1]]
    beside_rows = hops(sum(along_wide[-1:]), sum(along_narrow[1:][-1:]))
    early = len(rounds)
    total = None
    for i in range(max(early, 1)):
        begin, end = (i * slots // max(early, 1), (i + 1) * slots // max(early, 1))
        if end > begin:
            total = call(
                functools.partial(second_backward_kernel, begin, end),
                [whole],
                2,
                [counts, offsets, projected, probe_modes, sorted_weights, tables]
                + ([] if begin == 0 else [total]),
                [stage],
                pass_flops // 2 * (end - begin) // slots,
                {} if begin == 0 else {6: 0},
            )[0]
        sums = add_hops(sums, rounds[i : i + 1])
        if end > 0:
            total, sums = lax.optimization_barrier((total, sums))
    margin = shape(2 * blocks * HALO, 128)
    f1, f2 = call(send_margins_kernel, [margin, margin], 0, [total])
    f2, f1 = (swap(f2, "wide", 1), swap(f1, "wide", 0))
    middle, f1, f2, sums = call(
        fold_rows_kernel,
        [shape(2, blocks, rows, 128), shape(rows + 8, 128), shape(rows + 8, 128), shape(8, 128)],
        0,
        [f2, f1, total] + take_hops(sums, beside_rows),
    )
    f2, f1 = (swap(f2, "narrow", 1), swap(f1, "narrow", 0))
    solved, left_over = call(
        finish_kernel,
        [shape(2, rows, width)] * 2,
        0,
        [f2, f1, gradient, image, middle, sums],
        [pltpu.VMEM((2, rows, width), F32)] * 2 + [pltpu.SemaphoreType.DMA((2, 2))],
        out_far=True,
    )
    return (solved, left_over)


def solution(mesh):
    placed = (
        P(None, "wide", "narrow"),
        P(),
        P("wide", "narrow", None, None, None, None, None),
        P("wide", "narrow", None, None),
        P("wide", "narrow"),
    )
    return jax.shard_map(
        local,
        mesh=mesh,
        in_specs=placed,
        out_specs=(P(None, "wide", "narrow"), P(None, "wide", "narrow")),
        check_vma=False,
    )
```

```python
import functools
import math

import jax
import jax.numpy as jnp
import numpy as np
from jax import lax
from jax.experimental import pallas as pl
from jax.experimental.pallas import tpu as pltpu
from jax.sharding import PartitionSpec as P

HALO = 64
damping = 0.5
F32 = jnp.float32
BF16 = jnp.bfloat16
MIB = 1024 * 1024


def pairs(size, odd):
    found = []
    for i in range(odd, size - 1, 2):
        found += [(i, i + 1), (i + 1, i)]
    return found


def swap(x, axis, odd):
    wanted = pairs(lax.axis_size(axis), odd)
    if not wanted:
        return jnp.zeros_like(x)
    return lax.ppermute(x, axis, wanted)


def half_tables(length):
    counter = np.arange(length)
    angles = ((counter[:, None] * counter[None, :]) % length).astype(np.float32)
    angles = angles * np.float32(2.0 * math.pi / length)
    factor = np.float32(1.0 / math.sqrt(length))
    cos, sin = (np.cos(angles) * factor, np.sin(angles) * factor)
    half = length // 2
    tables = []
    for parity in (0, 1):
        c, s = (cos[parity::2, :half], sin[parity::2, :half])
        left = np.concatenate([np.concatenate([c, s], 1), np.concatenate([-s, c], 1)], 0)
        tables += [left, left.T]
    return jnp.asarray(np.stack(tables), BF16)


def sorting_tables(length):
    order = np.concatenate([np.arange(0, length, 2), np.arange(1, length, 2)])
    left = np.zeros((length, length), np.float32)
    left[np.arange(length), order] = 1.0
    return jnp.asarray(np.stack([left, left.T]), BF16)


def dot(a, b):
    return jnp.dot(a, b, preferred_element_type=F32)


def cat(parts, axis):
    return jnp.concatenate(parts, axis=axis)


def lanes_low(shape):
    return lax.broadcasted_iota(jnp.int32, shape, len(shape) - 1) < shape[-1] // 2


def shifted_place(frames, k, blocks):
    row = HALO + frames[1][0, k]
    col = frames[1][1, k]
    first = jnp.where(col < 0, blocks - 1, 0)
    places = [lax.rem(first + i, blocks) for i in range(blocks)]
    return (row, places, jnp.where(col < 0, col + 128, col))


def take_patch(ext, frames, k, patch):
    width = patch.shape[1]
    row, places, across = shifted_place(frames, k, ext.shape[1])
    lane = lax.broadcasted_iota(jnp.int32, (width, 128), 1)
    back = lax.rem(128 - across, 128)
    for q in range(2):
        found = [ext[q, place, pl.ds(row, width), :] for place in places]
        for i in range(width // 128):
            both = jnp.where(lane >= across, found[i], found[i + 1])
            patch[q, :, 128 * i : 128 * (i + 1)] = pltpu.roll(both, back, 1)


def put_patch(total, frames, k, parts):
    width = parts[0].shape[0]
    row, places, across = shifted_place(frames, k, total.shape[1])
    lane = lax.broadcasted_iota(jnp.int32, (width, 128), 1)
    none = jnp.zeros((width, 128), F32)
    for q in range(2):
        turned = [none]
        for i in range(width // 128):
            turned.append(pltpu.roll(parts[q][:, 128 * i : 128 * (i + 1)], across, 1))
        turned.append(none)
        for i, place in enumerate(places):
            total[q, place, pl.ds(row, width), :] += jnp.where(
                lane < across, turned[i], turned[i + 1]
            )


def project(patch, probe, weights, k, tables, stage):
    te, te_t, to, to_t = (tables[i] for i in range(4))
    xr, xi = (patch[0], patch[1])
    width = xr.shape[0]
    h = width // 2
    modes = probe.shape[0]
    for m in range(modes):
        pr, pi = (probe[m, 0].astype(F32), probe[m, 1].astype(F32))
        er, ei = (pr * xr - pi * xi, pr * xi + pi * xr)
        even = cat([er[:h] + er[h:], ei[:h] + ei[h:]], 0).astype(BF16)
        odd = cat([er[:h] - er[h:], ei[:h] - ei[h:]], 0).astype(BF16)
        for e, y in enumerate((dot(te, even), dot(to, odd))):
            yr, yi = (y[:h], y[h:])
            plus = cat([yr[:, :h] + yr[:, h:], yi[:, :h] + yi[:, h:]], 1)
            minus = cat([yr[:, :h] - yr[:, h:], yi[:, :h] - yi[:, h:]], 1)
            stage[0, m, e * h : (e + 1) * h] = plus.astype(BF16)
            stage[1, m, e * h : (e + 1) * h] = minus.astype(BF16)
    found = []
    for e, table in enumerate((te_t, to_t)):
        acc = None
        for m in range(modes):
            z = dot(stage[e, m], table)
            z = z * weights[k, m, :, e * width : (e + 1) * width].astype(F32)
            acc = z if m == 0 else acc + z
        found.append(acc[:, :h] + acc[:, h:])
    return tuple(found)


def back_project(pe, po, probe, weights, k, tables, stage):
    te, te_t, to, to_t = (tables[i] for i in range(4))
    width = pe.shape[0]
    h = width // 2
    modes = probe.shape[0]
    pe2, po2 = (cat([pe, pe], 1), cat([po, po], 1))
    for m in range(modes):
        ve = (weights[k, m, :, :width].astype(F32) * pe2).astype(BF16)
        vo = (weights[k, m, :, width:].astype(F32) * po2).astype(BF16)
        top = cat([cat([ve[:h, :h], vo[:h, :h]], 1), cat([ve[:h, h:], vo[:h, h:]], 1)], 0)
        low = cat([cat([ve[h:, :h], vo[h:, :h]], 1), cat([ve[h:, h:], vo[h:, h:]], 1)], 0)
        a, b = (dot(te_t, top), dot(to_t, low))
        s, d = (a + b, a - b)
        for e, c in enumerate((slice(0, h), slice(h, width))):
            stage[e, m, :h] = cat([s[:h, c], s[h:, c]], 1).astype(BF16)
            stage[e, m, h:] = cat([d[:h, c], d[h:, c]], 1).astype(BF16)
    cr = ci = None
    for m in range(modes):
        a, b = (dot(stage[0, m], te), dot(stage[1, m], to))
        s, d = (a + b, a - b)
        nr, ni = (cat([s[:, :h], d[:, :h]], 1), cat([s[:, h:], d[:, h:]], 1))
        pr, pi = (probe[m, 0].astype(F32), probe[m, 1].astype(F32))
        r = pr * nr + pi * ni
        i = pr * ni - pi * nr
        cr = r if m == 0 else cr + r
        ci = i if m == 0 else ci + i
    return (cr, ci)


def square_sum(x):
    return jnp.sum(x * x)


def scalar_tile(values):
    rows = lax.broadcasted_iota(jnp.int32, (8, 128), 0)
    tile = jnp.zeros((8, 128), F32)
    for i, value in enumerate(values):
        tile = jnp.where(rows == i, value, tile)
    return tile


def parity_of(axis):
    return lax.rem(lax.axis_index(axis), 2)


def by_parity(axis, low, high, first, second):
    even = parity_of(axis) == 0

    @pl.when(even)
    def _():
        first(high())
        second(low())

    @pl.when(jnp.logical_not(even))
    def _():
        first(low())
        second(high())


def lower_upper(axis, first, second):
    even = parity_of(axis) == 0
    return (jnp.where(even, second, first), jnp.where(even, first, second))


def store(ref):
    def put(value):
        ref[...] = value

    return put


def halo_kernel(g, row1, row2, col1, col2, ends, arrived):
    n, width = g.shape[1:]

    def move(source, to, i):
        return pltpu.make_async_copy(source, to, arrived.at[i])

    sides = [move(g.at[:, :, at : at + 128], ends.at[i], i) for i, at in enumerate((0, width - 128))]
    for side in sides:
        side.start()
    low, high = (g.at[:, :HALO], g.at[:, n - HALO :])
    by_parity(
        "wide",
        lambda: low,
        lambda: high,
        lambda source: move(source, row1, 2).start(),
        lambda source: move(source, row2, 3).start(),
    )
    for side in sides:
        side.wait()
    half = lanes_low(col1.shape)
    by_parity(
        "narrow",
        lambda: jnp.where(half, ends[0, 0], pltpu.roll(ends[0, 1], HALO, 1)),
        lambda: jnp.where(half, pltpu.roll(ends[1, 1], HALO, 1), ends[1, 0]),
        store(col1),
        store(col2),
    )
    move(low, row1, 2).wait()
    move(low, row2, 3).wait()


def fill_cols(put, first, second):
    left, right = lower_upper("narrow", first[...], second[...])
    low = lanes_low(right.shape)
    put(0, jnp.where(low, right, left))
    put(1, pltpu.roll(jnp.where(low, left, right), HALO, 1))


def corners_kernel(col2, col1, first, second, beside):
    n = beside.shape[1]

    def put(q, value):
        beside[q] = value

    fill_cols(put, col1, col2)
    by_parity(
        "wide",
        lambda: beside[:, :HALO],
        lambda: beside[:, n - HALO :],
        store(first),
        store(second),
    )


def fill_tile(ext, g, row1, row2, col1, col2, corner1, corner2):
    n, width = g.shape[1:]
    last = width // 128
    above, below = lower_upper("wide", row1[...], row2[...])
    for b in range(last):
        cols = slice(128 * b, 128 * (b + 1))
        ext[:, b, :HALO] = above[:, :, cols]
        ext[:, b, HALO : HALO + n] = g[:, :, cols]
        ext[:, b, HALO + n :] = below[:, :, cols]

    def put(q, value):
        ext[q, last, HALO : HALO + n] = value

    fill_cols(put, col1, col2)
    above, below = lower_upper("wide", corner1[...], corner2[...])
    ext[:, last, :HALO] = above
    ext[:, last, HALO + n :] = below


def sort_weights(frames, w, sorter, out, held, arrived, begin, end, meanwhile):
    width = w.shape[-1]
    h = width // 2
    modes = w.shape[1]

    def fetch(k):
        return pltpu.make_async_copy(w.at[k], held.at[k], arrived.at[k])

    for k in range(begin, end):

        @pl.when(k < frames[0][0])
        def _():
            fetch(k).start()

    meanwhile()

    def visit(k, carried):
        fetch(k).wait()
        for m in range(modes):
            for q in range(2):
                held[k, m, q] = dot(sorter[0], held[k, m, q]).astype(BF16)
        for m in range(modes):
            for q in range(2):
                x = dot(held[k, m, q], sorter[1]).astype(BF16)
                out[k, m, :, q * h : (q + 1) * h] = x[:, :h]
                out[k, m, :, width + q * h : width + (q + 1) * h] = x[:, h:]
        return carried

    lax.fori_loop(begin, jnp.minimum(end, frames[0][0]), visit, 0)


def prepare_kernel(
    counts, corner, w, sorter_far, probe_far, tables_far, g_far,
    out, probe, tables, g, held, sorter, arrived, loaded,
):
    frames = (counts, None)
    moves = ((sorter_far, sorter), (g_far, g), (probe_far, probe), (tables_far, tables))
    moves = [pltpu.make_async_copy(a, b, loaded.at[i]) for i, (a, b) in enumerate(moves)]
    moves[0].start()

    def meanwhile():
        for move in moves[1:]:
            move.start()
        moves[0].wait()

    sort_weights(frames, w, sorter, out, held, arrived, 0, w.shape[0], meanwhile)
    for move in moves[1:]:
        move.wait()


def first_pass_kernel(
    counts, offsets, row2, row1, g, col1, col2, corner1, corner2, probe, weights, tables,
    total, sums, sr1, sr2, si1, si2, ext, patch, stage,
):
    frames = (counts, offsets)
    fill_tile(ext, g, row1, row2, col1, col2, corner1, corner2)
    total[...] = jnp.zeros_like(total)

    def visit(k, energy):
        take_patch(ext, frames, k, patch)
        pe, po = project(patch, probe, weights, k, tables, stage)
        put_patch(total, frames, k, back_project(pe, po, probe, weights, k, tables, stage))
        return energy + square_sum(pe) + square_sum(po)

    energy = lax.fori_loop(0, frames[0][0], visit, F32(0.0))
    sums[...] = scalar_tile([square_sum(g[...]), energy])
    send_row_bands(total, 0, sr1, sr2)
    send_col_bands(total, 1, si1, si2)


def send_row_bands(total, q, first, second):
    n = total.shape[2]
    by_parity(
        "wide",
        lambda: total[q, :, : 2 * HALO].reshape(first.shape),
        lambda: total[q, :, n - 2 * HALO :].reshape(first.shape),
        store(first),
        store(second),
    )


def send_col_bands(total, q, first, second):
    last = total.shape[1] - 1
    low = lanes_low(first.shape)
    by_parity(
        "narrow",
        lambda: jnp.where(low, total[q, 0], total[q, last]),
        lambda: jnp.where(low, total[q, last], total[q, last - 1]),
        store(first),
        store(second),
    )


def add_row_bands(total, q, first, second):
    blocks, n = total.shape[1:3]
    above, below = lower_upper("wide", first[...], second[...])
    total[q, :, : 2 * HALO] += above.reshape(blocks, 2 * HALO, 128)
    total[q, :, n - 2 * HALO :] += below.reshape(blocks, 2 * HALO, 128)


def add_col_bands(total, q, first, second):
    last = total.shape[1] - 1
    left, right = lower_upper("narrow", first[...], second[...])
    low = lanes_low(right.shape)
    total[q, last] += jnp.where(low, right, left)
    total[q, 0] += jnp.where(low, left, 0.0)
    total[q, last - 1] += jnp.where(low, 0.0, right)


def bands_kernel(rr2, ri1, ri2, rr1, total, out, sr1, sr2, si1, si2):
    add_row_bands(out, 0, rr1, rr2)
    add_col_bands(out, 1, ri1, ri2)
    send_col_bands(out, 0, sr1, sr2)
    send_row_bands(out, 1, si1, si2)


def second_forward_kernel(
    last_row, last_col, counts, offsets, ri2, rr1, rr2, ri1, total, sums, probe, weights, tables,
    image, projected, all_sums, ext, patch, stage,
):
    frames = (counts, offsets)
    last = ext.shape[1] - 1
    n = ext.shape[2]
    ext[...] = total[...]
    add_col_bands(ext, 0, rr1, rr2)
    add_row_bands(ext, 1, ri1, ri2)

    @pl.when(lax.axis_index("wide") == 0)
    def _():
        ext[:, :, :HALO] = jnp.zeros((2, last + 1, HALO, 128), F32)

    @pl.when(lax.axis_index("wide") == last_row)
    def _():
        ext[:, :, n - HALO :] = jnp.zeros((2, last + 1, HALO, 128), F32)

    low = lanes_low((2, n, 128))

    @pl.when(lax.axis_index("narrow") == 0)
    def _():
        ext[:, last] = jnp.where(low, ext[:, last], 0.0)

    @pl.when(lax.axis_index("narrow") == last_col)
    def _():
        ext[:, last] = jnp.where(low, 0.0, ext[:, last])

    for b in range(last):
        image[:, :, 128 * b : 128 * (b + 1)] = ext[:, b, HALO : n - HALO]

    def visit(k, energy):
        take_patch(ext, frames, k, patch)
        pe, po = project(patch, probe, weights, k, tables, stage)
        projected[k] = cat([pe, po], 1)
        return energy + square_sum(pe) + square_sum(po)

    energy = lax.fori_loop(0, frames[0][0], visit, F32(0.0))
    rows = lax.broadcasted_iota(jnp.int32, (8, 128), 0)
    all_sums[...] = jnp.where(
        rows == 2, square_sum(image[...]), jnp.where(rows == 3, energy, sums[...])
    )


def second_backward_kernel(begin, end, counts, offsets, projected, probe, weights, tables, *rest):
    frames = (counts, offsets)
    total, stage = rest[-2:]
    h = projected.shape[2] // 2
    if begin == 0:
        total[...] = jnp.zeros_like(total)

    def visit(k, carried):
        pe, po = (projected[k, :, :h], projected[k, :, h:])
        parts = back_project(pe, po, probe, weights, k, tables, stage)
        put_patch(total, frames, k, parts)
        return carried

    lax.fori_loop(begin, jnp.minimum(end, frames[0][0]), visit, 0)


def send_margins_kernel(total, first, second):
    n = total.shape[2]
    by_parity(
        "wide",
        lambda: total[:, :, :HALO].reshape(first.shape),
        lambda: total[:, :, n - HALO :].reshape(first.shape),
        store(first),
        store(second),
    )


def fold_rows_kernel(second, first, total, *rest):
    parts, (middle, out_first, out_second, out_sums) = (rest[:-4], rest[-4:])
    blocks, n = middle.shape[1:3]
    last = blocks - 1
    above, below = lower_upper("wide", first[...], second[...])
    middle[...] = total[:, :, HALO : HALO + n]
    middle[:, :, :HALO] += above.reshape(2, blocks, HALO, 128)
    middle[:, :, n - HALO :] += below.reshape(2, blocks, HALO, 128)
    low = lanes_low((n, 128))
    re, im = (middle[0, last], pltpu.roll(middle[1, last], HALO, 1))
    by_parity(
        "narrow",
        lambda: jnp.where(low, im, re),
        lambda: jnp.where(low, re, im),
        store(out_first.at[:n]),
        store(out_second.at[:n]),
    )
    out_first[n:] = total_of(parts)
    out_second[n:] = out_first[n:]
    out_sums[...] = out_first[n:]


def finish_kernel(
    second, first, g, image, middle, sums, solved_out, left_out, solved, left_over, sent
):
    n, width = g.shape[1:]
    left, right = lower_upper("narrow", first[:n], second[:n])
    low = lanes_low(right.shape)
    total = sums[...] + first[n:]
    n0, s0, uu, s1 = (total[i : i + 1, :1] for i in range(4))
    mu = s0 / n0
    a0 = n0 / (s0 + damping * n0)
    n1 = a0 * a0 * (uu - mu * s0)
    b = n1 / n0
    c1 = a0 * mu + b
    curve = damping * (n1 + b * b * n0) + c1 * c1 * s0 - 2.0 * c1 * a0 * uu + a0 * a0 * s1
    a1 = n1 / curve
    last = width // 128 - 1
    for q in range(2):
        low_part = left if q == 0 else pltpu.roll(left, HALO, 1)
        high_part = right if q == 0 else pltpu.roll(right, HALO, 1)
        for block in range(last + 1):
            cols = slice(128 * block, 128 * (block + 1))
            v = middle[q, block]
            if block == 0:
                v = v + jnp.where(low, low_part, 0.0)
            if block == last:
                v = v + jnp.where(low, 0.0, high_part)
            x, u = (g[q, :, cols], image[q, :, cols])
            d1 = c1 * x - a0 * u
            solved[q, :, cols] = a0 * x + a1 * d1
            left_over[q, :, cols] = a0 * (mu * x - u) - a1 * (damping * d1 + c1 * u - a0 * v)
        for i, (value, to) in enumerate(((solved, solved_out), (left_over, left_out))):
            pltpu.make_async_copy(value.at[q], to.at[q], sent.at[q, i]).start()
    for q in range(2):
        for i, (value, to) in enumerate(((solved, solved_out), (left_over, left_out))):
            pltpu.make_async_copy(value.at[q], to.at[q], sent.at[q, i]).wait()


def total_of(refs):
    total = refs[0][...]
    for ref in refs[1:]:
        total = total + ref[...]
    return total


def add_kernel(*refs):
    refs[-1][...] = total_of(refs[:-1])


def hops(over_wide, over_narrow):
    rows, cols = (lax.axis_size("wide"), lax.axis_size("narrow"))
    pairs_of = [(down, right) for down in {0, over_wide} for right in {0, over_narrow}]
    return [
        [
            (i * cols + j, (i ^ down) * cols + (j ^ right))
            for i in range(rows)
            for j in range(cols)
        ]
        for down, right in sorted(pairs_of)
        if down or right
    ]


def powers(size):
    found = []
    while 2 ** len(found) < size:
        found.append(2 ** len(found))
    return found


def take_hops(x, wanted):
    return [x] + [lax.ppermute(x, ("wide", "narrow"), perm) for perm in wanted]


def add_hops(x, rounds):
    for wanted in rounds:
        x = call(add_kernel, [shape(8, 128)], 0, take_hops(x, wanted))[0]
    return x


def shape(*dims):
    return jax.ShapeDtypeStruct(dims, F32)


def call(kernel, outs, smem, args, scratch=(), flops=0, aliases={}, far=(), out_far=False):
    specs = [pl.BlockSpec(memory_space=pltpu.SMEM)] * smem
    specs += [pl.BlockSpec(memory_space=pltpu.VMEM)] * (len(args) - smem)
    for i in far:
        specs[i] = pl.BlockSpec(memory_space=pltpu.HBM)
    args = [
        arg if i < smem else pltpu.with_memory_space_constraint(arg, spec.memory_space)
        for i, (arg, spec) in enumerate(zip(args, specs))
    ]
    moved = sum(a.size * a.dtype.itemsize for a in args)
    moved += sum(math.prod(o.shape) * o.dtype.itemsize for o in outs)
    place = pltpu.HBM if out_far else pltpu.VMEM
    return pl.pallas_call(
        kernel,
        out_shape=[place(o.shape, o.dtype) for o in outs],
        in_specs=specs,
        out_specs=[pl.BlockSpec(memory_space=place)] * len(outs),
        scratch_shapes=list(scratch),
        input_output_aliases=aliases,
        compiler_params=pltpu.CompilerParams(vmem_limit_bytes=20 * MIB),
        cost_estimate=pl.CostEstimate(flops=flops, bytes_accessed=moved, transcendentals=0),
    )(*args)


def prepare(counts, corner, w, probe, tables, g):
    slots, modes, parts, rows, cols = w.shape
    sorter = sorting_tables(cols)
    weights = jax.ShapeDtypeStruct((slots, modes, rows, parts * cols), BF16)
    outs = [jax.ShapeDtypeStruct(x.shape, x.dtype) for x in (probe, tables, g)]
    scratch = [pltpu.VMEM(x.shape, BF16) for x in (w, sorter)]
    scratch += [pltpu.SemaphoreType.DMA((slots,)), pltpu.SemaphoreType.DMA((4,))]
    return call(
        prepare_kernel, [weights] + outs, 1, [counts, corner, w, sorter, probe, tables, g],
        scratch, 8 * slots * modes * rows * cols * rows, far=(2, 3, 4, 5, 6),
    )


def local(gradient, probe_modes, mode_weights, offsets, counts):
    weights = mode_weights[0, 0]
    slots, modes = weights.shape[:2]
    rows, width = gradient.shape[1:]
    tall, blocks = (rows + 2 * HALO, width // 128 + 1)
    counts = counts.reshape(-1)
    offsets = jnp.swapaxes(offsets, 2, 3).reshape(offsets.shape[3], offsets.shape[2])
    tables = half_tables(width)
    pass_flops = 8 * 2 * slots * modes * 2 * width * width * width
    extended = pltpu.VMEM((2, blocks, tall, 128), F32)
    patch = pltpu.VMEM((2, rows, width), F32)
    stage = pltpu.VMEM((2, modes, rows, width), BF16)
    whole = shape(2, blocks, tall, 128)

    row_strip, col_strip, corner = (shape(2, HALO, width), shape(rows, 128), shape(2, HALO, 128))
    row1, row2, col1, col2 = call(
        halo_kernel, [row_strip, row_strip, col_strip, col_strip], 0, [gradient],
        [pltpu.VMEM((2, 2, rows, 128), F32), pltpu.SemaphoreType.DMA((4,))], far=(0,),
    )
    col1, col2 = (swap(col1, "narrow", 0), swap(col2, "narrow", 1))
    row2, row1 = (swap(row2, "wide", 1), swap(row1, "wide", 0))
    corner1, corner2 = call(
        corners_kernel, [corner, corner], 0, [col2, col1], [pltpu.VMEM((2, rows, 128), F32)]
    )
    sorted_weights, probe_modes, tables, gradient = prepare(
        counts, corner1, weights, probe_modes, tables, gradient
    )
    corner2, corner1 = (swap(corner2, "wide", 1), swap(corner1, "wide", 0))

    row_band, col_band = (shape(blocks * 2 * HALO, 128), shape(tall, 128))
    total, sums, sr1, sr2, si1, si2 = call(
        first_pass_kernel,
        [whole, shape(8, 128), row_band, row_band, col_band, col_band],
        2,
        [
            counts, offsets, row2, row1, gradient, col1, col2, corner1, corner2,
            probe_modes, sorted_weights, tables,
        ],
        [extended, patch, stage],
        pass_flops,
    )
    sr2, si1, si2, sr1 = (
        swap(sr2, "wide", 1), swap(si1, "narrow", 0), swap(si2, "narrow", 1), swap(sr1, "wide", 0)
    )
    total, sr1, sr2, si1, si2 = call(
        bands_kernel,
        [whole, col_band, col_band, row_band, row_band],
        0,
        [sr2, si1, si2, sr1, total],
        aliases={4: 0},
    )
    si2, sr1, sr2, si1 = (
        swap(si2, "wide", 1), swap(sr1, "narrow", 0), swap(sr2, "narrow", 1), swap(si1, "wide", 0)
    )
    image, projected, sums = call(
        functools.partial(
            second_forward_kernel, lax.axis_size("wide") - 1, lax.axis_size("narrow") - 1
        ),
        [shape(2, rows, width), shape(slots, rows, width), shape(8, 128)],
        2,
        [
            counts, offsets, si2, sr1, sr2, si1, total, sums, probe_modes, sorted_weights, tables,
        ],
        [extended, patch, stage],
        pass_flops // 2,
    )
    along_wide, along_narrow = (powers(lax.axis_size("wide")), powers(lax.axis_size("narrow")))
    rounds = [hops(step, 0) for step in along_wide[:-1]]
    rounds += [hops(0, step) for step in along_narrow[1:-1]]
    beside_rows = hops(sum(along_wide[-1:]), sum(along_narrow[1:][-1:]))
    early = len(rounds)
    total = None
    for i in range(max(early, 1)):
        begin, end = (i * slots // max(early, 1), (i + 1) * slots // max(early, 1))
        if end > begin:
            total = call(
                functools.partial(second_backward_kernel, begin, end),
                [whole],
                2,
                [counts, offsets, projected, probe_modes, sorted_weights, tables]
                + ([] if begin == 0 else [total]),
                [stage],
                pass_flops // 2 * (end - begin) // slots,
                {} if begin == 0 else {6: 0},
            )[0]
        sums = add_hops(sums, rounds[i : i + 1])
        if end > 0:
            total, sums = lax.optimization_barrier((total, sums))
    margin = shape(2 * blocks * HALO, 128)
    f1, f2 = call(send_margins_kernel, [margin, margin], 0, [total])
    f2, f1 = (swap(f2, "wide", 1), swap(f1, "wide", 0))
    middle, f1, f2, sums = call(
        fold_rows_kernel,
        [shape(2, blocks, rows, 128), shape(rows + 8, 128), shape(rows + 8, 128), shape(8, 128)],
        0,
        [f2, f1, total] + take_hops(sums, beside_rows),
    )
    f2, f1 = (swap(f2, "narrow", 1), swap(f1, "narrow", 0))
    solved, left_over = call(
        finish_kernel,
        [shape(2, rows, width)] * 2,
        0,
        [f2, f1, gradient, image, middle, sums],
        [pltpu.VMEM((2, rows, width), F32)] * 2 + [pltpu.SemaphoreType.DMA((2, 2))],
        out_far=True,
    )
    return (solved, left_over)


def solution(mesh):
    placed = (
        P(None, "wide", "narrow"),
        P(),
        P("wide", "narrow", None, None, None, None, None),
        P("wide", "narrow", None, None),
        P("wide", "narrow"),
    )
    return jax.shard_map(
        local,
        mesh=mesh,
        in_specs=placed,
        out_specs=(P(None, "wide", "narrow"), P(None, "wide", "narrow")),
        check_vma=False,
    )
```

```python
import functools
import math

import jax
import jax.numpy as jnp
import numpy as np
from jax import lax
from jax.experimental import pallas as pl
from jax.experimental.pallas import tpu as pltpu
from jax.sharding import PartitionSpec as P

HALO = 64
damping = 0.5
F32 = jnp.float32
BF16 = jnp.bfloat16
MIB = 1024 * 1024


def pairs(size, odd):
    found = []
    for i in range(odd, size - 1, 2):
        found += [(i, i + 1), (i + 1, i)]
    return found


def swap(x, axis, odd):
    wanted = pairs(lax.axis_size(axis), odd)
    if not wanted:
        return jnp.zeros_like(x)
    return lax.ppermute(x, axis, wanted)


def half_tables(length):
    counter = np.arange(length)
    angles = ((counter[:, None] * counter[None, :]) % length).astype(np.float32)
    angles = angles * np.float32(2.0 * math.pi / length)
    factor = np.float32(1.0 / math.sqrt(length))
    cos, sin = (np.cos(angles) * factor, np.sin(angles) * factor)
    half = length // 2
    tables = []
    for parity in (0, 1):
        c, s = (cos[parity::2, :half], sin[parity::2, :half])
        left = np.concatenate([np.concatenate([c, s], 1), np.concatenate([-s, c], 1)], 0)
        tables += [left, left.T]
    return jnp.asarray(np.stack(tables), BF16)


def sorting_tables(length):
    order = np.concatenate([np.arange(0, length, 2), np.arange(1, length, 2)])
    left = np.zeros((length, length), np.float32)
    left[np.arange(length), order] = 1.0
    return jnp.asarray(np.stack([left, left.T]), BF16)


def dot(a, b):
    return jnp.dot(a, b, preferred_element_type=F32)


def cat(parts, axis):
    return jnp.concatenate(parts, axis=axis)


def lanes_low(shape):
    return lax.broadcasted_iota(jnp.int32, shape, len(shape) - 1) < shape[-1] // 2


def shifted_place(frames, k, blocks):
    row = HALO + frames[1][0, k]
    col = frames[1][1, k]
    first = jnp.where(col < 0, blocks - 1, 0)
    places = [lax.rem(first + i, blocks) for i in range(blocks)]
    return (row, places, jnp.where(col < 0, col + 128, col))


def take_patch(ext, frames, k, patch):
    width = patch.shape[1]
    row, places, across = shifted_place(frames, k, ext.shape[1])
    lane = lax.broadcasted_iota(jnp.int32, (width, 128), 1)
    back = lax.rem(128 - across, 128)
    for q in range(2):
        found = [ext[q, place, pl.ds(row, width), :] for place in places]
        for i in range(width // 128):
            both = jnp.where(lane >= across, found[i], found[i + 1])
            patch[q, :, 128 * i : 128 * (i + 1)] = pltpu.roll(both, back, 1)


def put_patch(total, frames, k, parts):
    width = parts[0].shape[0]
    row, places, across = shifted_place(frames, k, total.shape[1])
    lane = lax.broadcasted_iota(jnp.int32, (width, 128), 1)
    none = jnp.zeros((width, 128), F32)
    for q in range(2):
        turned = [none]
        for i in range(width // 128):
            turned.append(pltpu.roll(parts[q][:, 128 * i : 128 * (i + 1)], across, 1))
        turned.append(none)
        for i, place in enumerate(places):
            total[q, place, pl.ds(row, width), :] += jnp.where(
                lane < across, turned[i], turned[i + 1]
            )


def project(patch, probe, weights, k, tables, stage):
    te, te_t, to, to_t = (tables[i] for i in range(4))
    xr, xi = (patch[0], patch[1])
    width = xr.shape[0]
    h = width // 2
    modes = probe.shape[0]
    for m in range(modes):
        pr, pi = (probe[m, 0].astype(F32), probe[m, 1].astype(F32))
        er, ei = (pr * xr - pi * xi, pr * xi + pi * xr)
        even = cat([er[:h] + er[h:], ei[:h] + ei[h:]], 0).astype(BF16)
        odd = cat([er[:h] - er[h:], ei[:h] - ei[h:]], 0).astype(BF16)
        for e, y in enumerate((dot(te, even), dot(to, odd))):
            yr, yi = (y[:h], y[h:])
            plus = cat([yr[:, :h] + yr[:, h:], yi[:, :h] + yi[:, h:]], 1)
            minus = cat([yr[:, :h] - yr[:, h:], yi[:, :h] - yi[:, h:]], 1)
            stage[0, m, e * h : (e + 1) * h] = plus.astype(BF16)
            stage[1, m, e * h : (e + 1) * h] = minus.astype(BF16)
    found = []
    for e, table in enumerate((te_t, to_t)):
        acc = None
        for m in range(modes):
            z = dot(stage[e, m], table)
            z = z * weights[k, m, :, e * width : (e + 1) * width].astype(F32)
            acc = z if m == 0 else acc + z
        found.append(acc[:, :h] + acc[:, h:])
    return tuple(found)


def back_project(pe, po, probe, weights, k, tables, stage):
    te, te_t, to, to_t = (tables[i] for i in range(4))
    width = pe.shape[0]
    h = width // 2
    modes = probe.shape[0]
    pe2, po2 = (cat([pe, pe], 1), cat([po, po], 1))
    for m in range(modes):
        ve = (weights[k, m, :, :width].astype(F32) * pe2).astype(BF16)
        vo = (weights[k, m, :, width:].astype(F32) * po2).astype(BF16)
        top = cat([cat([ve[:h, :h], vo[:h, :h]], 1), cat([ve[:h, h:], vo[:h, h:]], 1)], 0)
        low = cat([cat([ve[h:, :h], vo[h:, :h]], 1), cat([ve[h:, h:], vo[h:, h:]], 1)], 0)
        a, b = (dot(te_t, top), dot(to_t, low))
        s, d = (a + b, a - b)
        for e, c in enumerate((slice(0, h), slice(h, width))):
            stage[e, m, :h] = cat([s[:h, c], s[h:, c]], 1).astype(BF16)
            stage[e, m, h:] = cat([d[:h, c], d[h:, c]], 1).astype(BF16)
    cr = ci = None
    for m in range(modes):
        a, b = (dot(stage[0, m], te), dot(stage[1, m], to))
        s, d = (a + b, a - b)
        nr, ni = (cat([s[:, :h], d[:, :h]], 1), cat([s[:, h:], d[:, h:]], 1))
        pr, pi = (probe[m, 0].astype(F32), probe[m, 1].astype(F32))
        r = pr * nr + pi * ni
        i = pr * ni - pi * nr
        cr = r if m == 0 else cr + r
        ci = i if m == 0 else ci + i
    return (cr, ci)


def square_sum(x):
    return jnp.sum(x * x)


def scalar_tile(values):
    rows = lax.broadcasted_iota(jnp.int32, (8, 128), 0)
    tile = jnp.zeros((8, 128), F32)
    for i, value in enumerate(values):
        tile = jnp.where(rows == i, value, tile)
    return tile


def parity_of(axis):
    return lax.rem(lax.axis_index(axis), 2)


def by_parity(axis, low, high, first, second):
    even = parity_of(axis) == 0

    @pl.when(even)
    def _():
        first(high())
        second(low())

    @pl.when(jnp.logical_not(even))
    def _():
        first(low())
        second(high())


def lower_upper(axis, first, second):
    even = parity_of(axis) == 0
    return (jnp.where(even, second, first), jnp.where(even, first, second))


def store(ref):
    def put(value):
        ref[...] = value

    return put


def halo_kernel(g, row1, row2, col1, col2, ends, arrived):
    n, width = g.shape[1:]

    def move(source, to, i):
        return pltpu.make_async_copy(source, to, arrived.at[i])

    sides = [move(g.at[:, :, at : at + 128], ends.at[i], i) for i, at in enumerate((0, width - 128))]
    for side in sides:
        side.start()
    low, high = (g.at[:, :HALO], g.at[:, n - HALO :])
    by_parity(
        "wide",
        lambda: low,
        lambda: high,
        lambda source: move(source, row1, 2).start(),
        lambda source: move(source, row2, 3).start(),
    )
    for side in sides:
        side.wait()
    half = lanes_low(col1.shape)
    by_parity(
        "narrow",
        lambda: jnp.where(half, ends[0, 0], pltpu.roll(ends[0, 1], HALO, 1)),
        lambda: jnp.where(half, pltpu.roll(ends[1, 1], HALO, 1), ends[1, 0]),
        store(col1),
        store(col2),
    )
    move(low, row1, 2).wait()
    move(low, row2, 3).wait()


def fill_cols(put, first, second):
    left, right = lower_upper("narrow", first[...], second[...])
    low = lanes_low(right.shape)
    put(0, jnp.where(low, right, left))
    put(1, pltpu.roll(jnp.where(low, left, right), HALO, 1))


def corners_kernel(col2, col1, first, second, beside):
    n = beside.shape[1]

    def put(q, value):
        beside[q] = value

    fill_cols(put, col1, col2)
    by_parity(
        "wide",
        lambda: beside[:, :HALO],
        lambda: beside[:, n - HALO :],
        store(first),
        store(second),
    )


def fill_tile(ext, g, row1, row2, col1, col2, corner1, corner2):
    n, width = g.shape[1:]
    last = width // 128
    above, below = lower_upper("wide", row1[...], row2[...])
    for b in range(last):
        cols = slice(128 * b, 128 * (b + 1))
        ext[:, b, :HALO] = above[:, :, cols]
        ext[:, b, HALO : HALO + n] = g[:, :, cols]
        ext[:, b, HALO + n :] = below[:, :, cols]

    def put(q, value):
        ext[q, last, HALO : HALO + n] = value

    fill_cols(put, col1, col2)
    above, below = lower_upper("wide", corner1[...], corner2[...])
    ext[:, last, :HALO] = above
    ext[:, last, HALO + n :] = below


def sort_weights(frames, w, sorter, out, held, arrived, begin, end, meanwhile):
    width = w.shape[-1]
    h = width // 2
    modes = w.shape[1]

    def fetch(k):
        return pltpu.make_async_copy(w.at[k], held.at[k], arrived.at[k])

    for k in range(begin, end):

        @pl.when(k < frames[0][0])
        def _():
            fetch(k).start()

    meanwhile()

    def visit(k, carried):
        fetch(k).wait()
        for m in range(modes):
            for q in range(2):
                held[k, m, q] = dot(sorter[0], held[k, m, q]).astype(BF16)
        for m in range(modes):
            for q in range(2):
                x = dot(held[k, m, q], sorter[1]).astype(BF16)
                out[k, m, :, q * h : (q + 1) * h] = x[:, :h]
                out[k, m, :, width + q * h : width + (q + 1) * h] = x[:, h:]
        return carried

    lax.fori_loop(begin, jnp.minimum(end, frames[0][0]), visit, 0)


def prepare_kernel(
    counts, corner, w, sorter_far, probe_far, tables_far, g_far,
    out, probe, tables, g, held, sorter, arrived, loaded,
):
    frames = (counts, None)
    moves = ((sorter_far, sorter), (g_far, g), (probe_far, probe), (tables_far, tables))
    moves = [pltpu.make_async_copy(a, b, loaded.at[i]) for i, (a, b) in enumerate(moves)]
    moves[0].start()

    def meanwhile():
        for move in moves[1:]:
            move.start()
        moves[0].wait()

    sort_weights(frames, w, sorter, out, held, arrived, 0, w.shape[0], meanwhile)
    for move in moves[1:]:
        move.wait()


def first_pass_kernel(
    counts, offsets, row2, row1, g, col1, col2, corner1, corner2, probe, weights, tables,
    total, sums, sr1, sr2, si1, si2, ext, patch, stage,
):
    frames = (counts, offsets)
    fill_tile(ext, g, row1, row2, col1, col2, corner1, corner2)
    total[...] = jnp.zeros_like(total)

    def visit(k, energy):
        take_patch(ext, frames, k, patch)
        pe, po = project(patch, probe, weights, k, tables, stage)
        put_patch(total, frames, k, back_project(pe, po, probe, weights, k, tables, stage))
        return energy + square_sum(pe) + square_sum(po)

    energy = lax.fori_loop(0, frames[0][0], visit, F32(0.0))
    sums[...] = scalar_tile([square_sum(g[...]), energy])
    send_row_bands(total, 0, sr1, sr2)
    send_col_bands(total, 1, si1, si2)


def send_row_bands(total, q, first, second):
    n = total.shape[2]
    by_parity(
        "wide",
        lambda: total[q, :, : 2 * HALO].reshape(first.shape),
        lambda: total[q, :, n - 2 * HALO :].reshape(first.shape),
        store(first),
        store(second),
    )


def send_col_bands(total, q, first, second):
    last = total.shape[1] - 1
    low = lanes_low(first.shape)
    by_parity(
        "narrow",
        lambda: jnp.where(low, total[q, 0], total[q, last]),
        lambda: jnp.where(low, total[q, last], total[q, last - 1]),
        store(first),
        store(second),
    )


def add_row_bands(total, q, first, second):
    blocks, n = total.shape[1:3]
    above, below = lower_upper("wide", first[...], second[...])
    total[q, :, : 2 * HALO] += above.reshape(blocks, 2 * HALO, 128)
    total[q, :, n - 2 * HALO :] += below.reshape(blocks, 2 * HALO, 128)


def add_col_bands(total, q, first, second):
    last = total.shape[1] - 1
    left, right = lower_upper("narrow", first[...], second[...])
    low = lanes_low(right.shape)
    total[q, last] += jnp.where(low, right, left)
    total[q, 0] += jnp.where(low, left, 0.0)
    total[q, last - 1] += jnp.where(low, 0.0, right)


def bands_kernel(rr2, ri1, ri2, rr1, total, out, sr1, sr2, si1, si2):
    add_row_bands(out, 0, rr1, rr2)
    add_col_bands(out, 1, ri1, ri2)
    send_col_bands(out, 0, sr1, sr2)
    send_row_bands(out, 1, si1, si2)


def second_forward_kernel(
    last_row, last_col, counts, offsets, ri2, rr1, rr2, ri1, total, sums, probe, weights, tables,
    image, projected, all_sums, ext, patch, stage,
):
    frames = (counts, offsets)
    last = ext.shape[1] - 1
    n = ext.shape[2]
    add_col_bands(ext, 0, rr1, rr2)
    add_row_bands(ext, 1, ri1, ri2)

    @pl.when(lax.axis_index("wide") == 0)
    def _():
        ext[:, :, :HALO] = jnp.zeros((2, last + 1, HALO, 128), F32)

    @pl.when(lax.axis_index("wide") == last_row)
    def _():
        ext[:, :, n - HALO :] = jnp.zeros((2, last + 1, HALO, 128), F32)

    low = lanes_low((2, n, 128))

    @pl.when(lax.axis_index("narrow") == 0)
    def _():
        ext[:, last] = jnp.where(low, ext[:, last], 0.0)

    @pl.when(lax.axis_index("narrow") == last_col)
    def _():
        ext[:, last] = jnp.where(low, 0.0, ext[:, last])

    for b in range(last):
        image[:, :, 128 * b : 128 * (b + 1)] = ext[:, b, HALO : n - HALO]

    def visit(k, energy):
        take_patch(ext, frames, k, patch)
        pe, po = project(patch, probe, weights, k, tables, stage)
        projected[k] = cat([pe, po], 1)
        return energy + square_sum(pe) + square_sum(po)

    energy = lax.fori_loop(0, frames[0][0], visit, F32(0.0))
    rows = lax.broadcasted_iota(jnp.int32, (8, 128), 0)
    all_sums[...] = jnp.where(
        rows == 2, square_sum(image[...]), jnp.where(rows == 3, energy, sums[...])
    )


def second_backward_kernel(begin, end, counts, offsets, projected, probe, weights, tables, *rest):
    frames = (counts, offsets)
    total, stage = rest[-2:]
    h = projected.shape[2] // 2
    if begin == 0:
        total[...] = jnp.zeros_like(total)

    def visit(k, carried):
        pe, po = (projected[k, :, :h], projected[k, :, h:])
        parts = back_project(pe, po, probe, weights, k, tables, stage)
        put_patch(total, frames, k, parts)
        return carried

    lax.fori_loop(begin, jnp.minimum(end, frames[0][0]), visit, 0)


def send_margins_kernel(total, first, second):
    n = total.shape[2]
    by_parity(
        "wide",
        lambda: total[:, :, :HALO].reshape(first.shape),
        lambda: total[:, :, n - HALO :].reshape(first.shape),
        store(first),
        store(second),
    )


def fold_rows_kernel(second, first, total, *rest):
    parts, (middle, out_first, out_second, out_sums) = (rest[:-4], rest[-4:])
    blocks, n = middle.shape[1:3]
    last = blocks - 1
    above, below = lower_upper("wide", first[...], second[...])
    middle[...] = total[:, :, HALO : HALO + n]
    middle[:, :, :HALO] += above.reshape(2, blocks, HALO, 128)
    middle[:, :, n - HALO :] += below.reshape(2, blocks, HALO, 128)
    low = lanes_low((n, 128))
    re, im = (middle[0, last], pltpu.roll(middle[1, last], HALO, 1))
    by_parity(
        "narrow",
        lambda: jnp.where(low, im, re),
        lambda: jnp.where(low, re, im),
        store(out_first.at[:n]),
        store(out_second.at[:n]),
    )
    out_first[n:] = total_of(parts)
    out_second[n:] = out_first[n:]
    out_sums[...] = out_first[n:]


def finish_kernel(
    second, first, g, image, middle, sums, solved_out, left_out, solved, left_over, sent
):
    n, width = g.shape[1:]
    left, right = lower_upper("narrow", first[:n], second[:n])
    low = lanes_low(right.shape)
    total = sums[...] + first[n:]
    n0, s0, uu, s1 = (total[i : i + 1, :1] for i in range(4))
    mu = s0 / n0
    a0 = n0 / (s0 + damping * n0)
    n1 = a0 * a0 * (uu - mu * s0)
    b = n1 / n0
    c1 = a0 * mu + b
    curve = damping * (n1 + b * b * n0) + c1 * c1 * s0 - 2.0 * c1 * a0 * uu + a0 * a0 * s1
    a1 = n1 / curve
    last = width // 128 - 1
    for q in range(2):
        low_part = left if q == 0 else pltpu.roll(left, HALO, 1)
        high_part = right if q == 0 else pltpu.roll(right, HALO, 1)
        for block in range(last + 1):
            cols = slice(128 * block, 128 * (block + 1))
            v = middle[q, block]
            if block == 0:
                v = v + jnp.where(low, low_part, 0.0)
            if block == last:
                v = v + jnp.where(low, 0.0, high_part)
            x, u = (g[q, :, cols], image[q, :, cols])
            d1 = c1 * x - a0 * u
            solved[q, :, cols] = a0 * x + a1 * d1
            left_over[q, :, cols] = a0 * (mu * x - u) - a1 * (damping * d1 + c1 * u - a0 * v)
        for i, (value, to) in enumerate(((solved, solved_out), (left_over, left_out))):
            pltpu.make_async_copy(value.at[q], to.at[q], sent.at[q, i]).start()
    for q in range(2):
        for i, (value, to) in enumerate(((solved, solved_out), (left_over, left_out))):
            pltpu.make_async_copy(value.at[q], to.at[q], sent.at[q, i]).wait()


def total_of(refs):
    total = refs[0][...]
    for ref in refs[1:]:
        total = total + ref[...]
    return total


def add_kernel(*refs):
    refs[-1][...] = total_of(refs[:-1])


def hops(over_wide, over_narrow):
    rows, cols = (lax.axis_size("wide"), lax.axis_size("narrow"))
    pairs_of = [(down, right) for down in {0, over_wide} for right in {0, over_narrow}]
    return [
        [
            (i * cols + j, (i ^ down) * cols + (j ^ right))
            for i in range(rows)
            for j in range(cols)
        ]
        for down, right in sorted(pairs_of)
        if down or right
    ]


def powers(size):
    found = []
    while 2 ** len(found) < size:
        found.append(2 ** len(found))
    return found


def take_hops(x, wanted):
    return [x] + [lax.ppermute(x, ("wide", "narrow"), perm) for perm in wanted]


def add_hops(x, rounds):
    for wanted in rounds:
        x = call(add_kernel, [shape(8, 128)], 0, take_hops(x, wanted))[0]
    return x


def shape(*dims):
    return jax.ShapeDtypeStruct(dims, F32)


def call(kernel, outs, smem, args, scratch=(), flops=0, aliases={}, far=(), out_far=False):
    specs = [pl.BlockSpec(memory_space=pltpu.SMEM)] * smem
    specs += [pl.BlockSpec(memory_space=pltpu.VMEM)] * (len(args) - smem)
    for i in far:
        specs[i] = pl.BlockSpec(memory_space=pltpu.HBM)
    args = [
        arg if i < smem else pltpu.with_memory_space_constraint(arg, spec.memory_space)
        for i, (arg, spec) in enumerate(zip(args, specs))
    ]
    moved = sum(a.size * a.dtype.itemsize for a in args)
    moved += sum(math.prod(o.shape) * o.dtype.itemsize for o in outs)
    place = pltpu.HBM if out_far else pltpu.VMEM
    return pl.pallas_call(
        kernel,
        out_shape=[place(o.shape, o.dtype) for o in outs],
        in_specs=specs,
        out_specs=[pl.BlockSpec(memory_space=place)] * len(outs),
        scratch_shapes=list(scratch),
        input_output_aliases=aliases,
        compiler_params=pltpu.CompilerParams(vmem_limit_bytes=20 * MIB),
        cost_estimate=pl.CostEstimate(flops=flops, bytes_accessed=moved, transcendentals=0),
    )(*args)


def prepare(counts, corner, w, probe, tables, g):
    slots, modes, parts, rows, cols = w.shape
    sorter = sorting_tables(cols)
    weights = jax.ShapeDtypeStruct((slots, modes, rows, parts * cols), BF16)
    outs = [jax.ShapeDtypeStruct(x.shape, x.dtype) for x in (probe, tables, g)]
    scratch = [pltpu.VMEM(x.shape, BF16) for x in (w, sorter)]
    scratch += [pltpu.SemaphoreType.DMA((slots,)), pltpu.SemaphoreType.DMA((4,))]
    return call(
        prepare_kernel, [weights] + outs, 1, [counts, corner, w, sorter, probe, tables, g],
        scratch, 8 * slots * modes * rows * cols * rows, far=(2, 3, 4, 5, 6),
    )


def local(gradient, probe_modes, mode_weights, offsets, counts):
    weights = mode_weights[0, 0]
    slots, modes = weights.shape[:2]
    rows, width = gradient.shape[1:]
    tall, blocks = (rows + 2 * HALO, width // 128 + 1)
    counts = counts.reshape(-1)
    offsets = jnp.swapaxes(offsets, 2, 3).reshape(offsets.shape[3], offsets.shape[2])
    tables = half_tables(width)
    pass_flops = 8 * 2 * slots * modes * 2 * width * width * width
    extended = pltpu.VMEM((2, blocks, tall, 128), F32)
    patch = pltpu.VMEM((2, rows, width), F32)
    stage = pltpu.VMEM((2, modes, rows, width), BF16)
    whole = shape(2, blocks, tall, 128)

    row_strip, col_strip, corner = (shape(2, HALO, width), shape(rows, 128), shape(2, HALO, 128))
    row1, row2, col1, col2 = call(
        halo_kernel, [row_strip, row_strip, col_strip, col_strip], 0, [gradient],
        [pltpu.VMEM((2, 2, rows, 128), F32), pltpu.SemaphoreType.DMA((4,))], far=(0,),
    )
    col1, col2 = (swap(col1, "narrow", 0), swap(col2, "narrow", 1))
    row2, row1 = (swap(row2, "wide", 1), swap(row1, "wide", 0))
    corner1, corner2 = call(
        corners_kernel, [corner, corner], 0, [col2, col1], [pltpu.VMEM((2, rows, 128), F32)]
    )
    sorted_weights, probe_modes, tables, gradient = prepare(
        counts, corner1, weights, probe_modes, tables, gradient
    )
    corner2, corner1 = (swap(corner2, "wide", 1), swap(corner1, "wide", 0))

    row_band, col_band = (shape(blocks * 2 * HALO, 128), shape(tall, 128))
    total, sums, sr1, sr2, si1, si2 = call(
        first_pass_kernel,
        [whole, shape(8, 128), row_band, row_band, col_band, col_band],
        2,
        [
            counts, offsets, row2, row1, gradient, col1, col2, corner1, corner2,
            probe_modes, sorted_weights, tables,
        ],
        [extended, patch, stage],
        pass_flops,
    )
    sr2, si1, si2, sr1 = (
        swap(sr2, "wide", 1), swap(si1, "narrow", 0), swap(si2, "narrow", 1), swap(sr1, "wide", 0)
    )
    total, sr1, sr2, si1, si2 = call(
        bands_kernel,
        [whole, col_band, col_band, row_band, row_band],
        0,
        [sr2, si1, si2, sr1, total],
        aliases={4: 0},
    )
    si2, sr1, sr2, si1 = (
        swap(si2, "wide", 1), swap(sr1, "narrow", 0), swap(sr2, "narrow", 1), swap(si1, "wide", 0)
    )
    image, projected, sums, _ = call(
        functools.partial(
            second_forward_kernel, lax.axis_size("wide") - 1, lax.axis_size("narrow") - 1
        ),
        [shape(2, rows, width), shape(slots, rows, width), shape(8, 128), whole],
        2,
        [
            counts, offsets, si2, sr1, sr2, si1, total, sums, probe_modes, sorted_weights, tables,
        ],
        [patch, stage],
        pass_flops // 2,
        {6: 3},
    )
    along_wide, along_narrow = (powers(lax.axis_size("wide")), powers(lax.axis_size("narrow")))
    rounds = [hops(step, 0) for step in along_wide[:-1]]
    rounds += [hops(0, step) for step in along_narrow[1:-1]]
    beside_rows = hops(sum(along_wide[-1:]), sum(along_narrow[1:][-1:]))
    early = len(rounds)
    total = None
    for i in range(max(early, 1)):
        begin, end = (i * slots // max(early, 1), (i + 1) * slots // max(early, 1))
        if end > begin:
            total = call(
                functools.partial(second_backward_kernel, begin, end),
                [whole],
                2,
                [counts, offsets, projected, probe_modes, sorted_weights, tables]
                + ([] if begin == 0 else [total]),
                [stage],
                pass_flops // 2 * (end - begin) // slots,
                {} if begin == 0 else {6: 0},
            )[0]
        sums = add_hops(sums, rounds[i : i + 1])
        if end > 0:
            total, sums = lax.optimization_barrier((total, sums))
    margin = shape(2 * blocks * HALO, 128)
    f1, f2 = call(send_margins_kernel, [margin, margin], 0, [total])
    f2, f1 = (swap(f2, "wide", 1), swap(f1, "wide", 0))
    middle, f1, f2, sums = call(
        fold_rows_kernel,
        [shape(2, blocks, rows, 128), shape(rows + 8, 128), shape(rows + 8, 128), shape(8, 128)],
        0,
        [f2, f1, total] + take_hops(sums, beside_rows),
    )
    f2, f1 = (swap(f2, "narrow", 1), swap(f1, "narrow", 0))
    solved, left_over = call(
        finish_kernel,
        [shape(2, rows, width)] * 2,
        0,
        [f2, f1, gradient, image, middle, sums],
        [pltpu.VMEM((2, rows, width), F32)] * 2 + [pltpu.SemaphoreType.DMA((2, 2))],
        out_far=True,
    )
    return (solved, left_over)


def solution(mesh):
    placed = (
        P(None, "wide", "narrow"),
        P(),
        P("wide", "narrow", None, None, None, None, None),
        P("wide", "narrow", None, None),
        P("wide", "narrow"),
    )
    return jax.shard_map(
        local,
        mesh=mesh,
        in_specs=placed,
        out_specs=(P(None, "wide", "narrow"), P(None, "wide", "narrow")),
        check_vma=False,
    )
```
